128 devices in a mesh: row: 8 (over y_lo, z), col: 16 (over x, y_hi, core).
Axes of the slice: x: 4, y: 4 (y_hi: 2, y_lo: 2; y = y_hi * 2 + y_lo), z: 4, core: 2. Of those that a mesh axis runs over, the one named last changes fastest.
Arguments:
- x_blocks: bfloat16 [2048, 2048, 128], P('row', 'col'), may hold values from -0.046875 to 0.046875
- block_ids: int32 [2048, 16], P('row', 'col'), may hold values from 0 to 511, as said below
- margins: float32 [32768], P('row'), may hold values from -6 to 6
- deleted: int32 [4096], P('row'), may hold values from 0 to 32767, as said below
- grads: float32 [32768, 128], P('col'), may hold values from -6 to 6
Outputs:
- solution: float32 [32768, 128], P('col')
- residual: float32 [32768, 128], P('col')
The draws below stay inside these ranges and needn't reach their ends.
Inputs may be any that keep to these rules, and one draw needn't show every extreme that they name: `block_ids`: each device's 256 entries are distinct and rise; each device lists the first and the last block of its grid. `deleted`: the 512 entries of row shard r are distinct rows of that shard, r * 4096 and up; each shard deletes its first and its last row.
All inputs are finite; a program needn't handle non-finite values.
Results may differ from the reference program's by a relative error of at most 0.015.
Values may be sent and summed in bfloat16 or wider, within the bound.
A program may use at most 128 MiB of HBM per device.

```python
import jax
import jax.numpy as jnp
from jax import lax

BLK = 128
DIRS = 128
ITERS = 3
RB = 32
FB = 16
NBLK = 256
DEL_DEV = 512
ROWS_DEV = 4096
FEAT_DEV = 2048
ROWS = 32768
FEATURES = 32768
BLOCKS_R = 2048
PANEL = 2048
N_ROW = 8
N_COL = 16


def draw_block_ids(key, part):
    row_shards = ROWS // ROWS_DEV
    column_shards = FEATURES // FEAT_DEV
    subkeys = jax.random.split(key, row_shards * column_shards)

    def choose(subkey):
        inner = jax.random.permutation(subkey, RB * FB - 2)[:NBLK - 2] + 1
        ends = jnp.array([0, RB * FB - 1], dtype=inner.dtype)
        return jnp.sort(jnp.concatenate([ends, inner]))
    chosen = jax.vmap(choose)(subkeys).reshape(row_shards, column_shards, NBLK)
    return jnp.transpose(chosen, (0, 2, 1)).reshape(row_shards * NBLK, column_shards).astype(jnp.int32)


def draw_deleted(key, part):
    row_shards = ROWS // ROWS_DEV
    subkeys = jax.random.split(key, row_shards)

    def choose(subkey):
        inner = jax.random.permutation(subkey, ROWS_DEV - 2)[:DEL_DEV - 2] + 1
        ends = jnp.array([0, ROWS_DEV - 1], dtype=inner.dtype)
        return jnp.concatenate([ends, inner])
    chosen = jax.vmap(choose)(subkeys)
    offsets = (jnp.arange(row_shards) * ROWS_DEV)[:, None]
    return (chosen + offsets).reshape(-1).astype(jnp.int32)


def draw_grads(key, part):
    key_base = jax.random.fold_in(key, 11)
    key_rows = jax.random.fold_in(key, 12)
    key_cols = jax.random.fold_in(key, 13)
    row_scale = jnp.exp(jax.random.uniform(key_rows, (FEATURES, 1), jnp.float32, jnp.log(0.1), 0.0))
    column_scale = jnp.exp(jax.random.uniform(key_cols, (1, DIRS), jnp.float32, jnp.log(0.3), 0.0))
    base = jax.random.normal(key_base, (FEATURES, DIRS), jnp.float32)
    return (jnp.clip(base, -6.0, 6.0) * row_scale * column_scale).astype(jnp.float32)


def block_levels(key, dims, pieces, least, high):
    loudness, own = 1.0, jax.random.fold_in(key, 6)
    for position, blocks in pieces:
        draws = jnp.exp(jax.random.uniform(jax.random.fold_in(own, position), (blocks,), jnp.float32, least / len(pieces), high / len(pieces)))
        loudness = loudness * jnp.repeat(draws, dims[position] // blocks).reshape([-1 if axis == position else 1 for axis in range(len(dims))])
    return loudness


def gaussian(key, shape, width, bound, shards=(), held_as=jnp.bfloat16):
    gain = block_levels(key, shape, shards, -0.22, 0.18) if shards else 1.0
    drawn = jax.random.normal(key, shape, jnp.float32) * width * gain
    return jnp.minimum(jnp.maximum(drawn, -bound), bound).astype(held_as)


def setup_inputs(seed: int = 0) -> dict:
    seeds = jax.random.split(jax.random.key(seed), 6)
    x_blocks = gaussian(seeds[0], (BLOCKS_R, PANEL, BLK), (NBLK * PANEL // RB) ** -0.5, 0.046875, ((0, 8), (1, 16)))
    block_ids = draw_block_ids(jax.random.fold_in(seeds[5], 71), 0)
    margins = gaussian(seeds[2], (ROWS,), 1.5, 6.0, ((0, 8),), jnp.float32)
    deleted = draw_deleted(jax.random.fold_in(seeds[5], 71), 0)
    grads = draw_grads(jax.random.fold_in(seeds[5], 71), 0)
    return dict(x_blocks=x_blocks, block_ids=block_ids, margins=margins, deleted=deleted, grads=grads)


highest = lax.Precision.HIGHEST
ridge_weight = 0.2


def forward_part(blocks, pattern, picked_tiles):
    block_row = pattern // FB
    block_column = pattern % FB
    gathered = picked_tiles[block_column].astype(jnp.float32)
    product = jnp.einsum("bij,bjk->bik", blocks.astype(jnp.float32), gathered, precision=highest)
    select = (block_row[:, None] == jnp.arange(RB, dtype=jnp.int32)[None, :]).astype(jnp.float32)
    return jnp.einsum("br,bik->rik", select, product, precision=highest)


def backward_part(blocks, pattern, scaled):
    block_row = pattern // FB
    block_column = pattern % FB
    gathered = scaled[block_row].astype(jnp.float32)
    product = jnp.einsum("bji,bjk->bik", blocks.astype(jnp.float32), gathered, precision=highest)
    select = (block_column[:, None] == jnp.arange(FB, dtype=jnp.int32)[None, :]).astype(jnp.float32)
    return jnp.einsum("bc,bik->cik", select, product, precision=highest)


def reference(x_blocks, block_ids, margins, deleted, grads):
    blocks = x_blocks.reshape(N_ROW, NBLK, N_COL, BLK, BLK)
    pattern = block_ids.reshape(N_ROW, NBLK, N_COL)
    shard_rows = jnp.arange(ROWS, dtype=jnp.int32).reshape(N_ROW, ROWS_DEV)
    dropped = deleted.reshape(N_ROW, DEL_DEV)
    removed = jnp.any(shard_rows[:, :, None] == dropped[:, None, :], axis=2)
    logistic = jax.nn.sigmoid(margins.reshape(N_ROW, ROWS_DEV))
    weights = jnp.where(removed, 0.0, logistic * (1.0 - logistic)).reshape(N_ROW, RB, BLK, 1)

    def operate(direction):
        picked_tiles = direction.astype(jnp.bfloat16).reshape(N_COL, FB, BLK, DIRS)

        def row_shard(row_index):
            def add_column(column_index, total):
                return total + forward_part(blocks[row_index, :, column_index], pattern[row_index, :, column_index], picked_tiles[column_index])
            return lax.fori_loop(0, N_COL, add_column, jnp.zeros((RB, BLK, DIRS), jnp.float32))

        projected = lax.map(row_shard, jnp.arange(N_ROW, dtype=jnp.int32))
        scaled = (weights * projected).astype(jnp.bfloat16)

        def column_shard(column_index):
            def add_row(row_index, total):
                return total + backward_part(blocks[row_index, :, column_index], pattern[row_index, :, column_index], scaled[row_index])
            return lax.fori_loop(0, N_ROW, add_row, jnp.zeros((FB, BLK, DIRS), jnp.float32))

        backward = lax.map(column_shard, jnp.arange(N_COL, dtype=jnp.int32)).reshape(FEATURES, DIRS)
        return backward + ridge_weight * direction

    solution = jnp.zeros_like(grads)
    residual = grads
    direction = grads
    norm_now = jnp.sum(residual * residual, axis=0)
    for iteration in range(ITERS):
        hessian_image = operate(direction)
        curvature = jnp.sum(direction * hessian_image, axis=0)
        step_size = norm_now / curvature
        solution = solution + step_size * direction
        residual = residual - step_size * hessian_image
        norm_next = jnp.sum(residual * residual, axis=0)
        direction = residual + (norm_next / norm_now) * direction
        norm_now = norm_next
    return solution, residual
```

```python
import functools

import jax
import jax.numpy as jnp
from jax import lax
from jax.experimental import pallas as pl
from jax.experimental.pallas import tpu as pltpu
from jax.sharding import PartitionSpec as P

ITERS = 3
RIDGE = 0.2
N_ROW, N_COL, N_CHIP = 8, 16, 8
BLK, DIRS, FB, RB, NBLK = 128, 128, 16, 32, 256
PIECE = 256
f32, bf16 = jnp.float32, jnp.bfloat16
MESH = pl.DeviceIdType.MESH


def tile(x, table, j, p, across):
    at = lambda a, b: x[table[(2 * j + a) * FB + 2 * p + b]]
    if across:
        top = jnp.concatenate([at(0, 0), at(1, 0)], axis=1)
        low = jnp.concatenate([at(0, 1), at(1, 1)], axis=1)
    else:
        top = jnp.concatenate([at(0, 0), at(0, 1)], axis=1)
        low = jnp.concatenate([at(1, 0), at(1, 1)], axis=1)
    return jnp.concatenate([top, low], axis=0)


def dot(a, b):
    return jnp.dot(a, b, preferred_element_type=f32)


def total(product):
    return jnp.sum((product[:, :BLK] + product[:, BLK:]).T, axis=0, keepdims=True)


def spread(row):
    square = jnp.broadcast_to(row, (DIRS, DIRS)).T
    return jnp.concatenate([square, square], axis=1)


def kernel(
    table, weights, grads, x_hbm, sol, res,
    x, xt, d, v, psend, prec, pown, csend, crec, s, acc, isend, irec, u,
    sc1, sc2, rr, coef,
    xsem, ps, pr, cs, cr, fs, fr, ss, sr, ims, imr, us, ur, s1s, s1r, s2s, s2r,
):
    r, c = lax.axis_index("row"), lax.axis_index("col")
    q, k = c // 2, c % 2
    sibling = (r, q * 2 + 1 - k)

    def chip(o):
        return ((q // 2 + o // 2) % 4) * 2 + (q % 2 + o % 2) % 2

    def chip_from(o):
        return ((q // 2 + 4 - o // 2) % 4) * 2 + (q % 2 + o % 2) % 2

    def rowdev(o):
        return ((r // 4 + o // 4) % 2) * 4 + (r % 4 + o % 4) % 4

    def rowdev_from(o):
        return ((r // 4 + o // 4) % 2) * 4 + (r % 4 + 4 - o % 4) % 4

    def remote(src, dst, send, recv, to):
        return pltpu.make_async_remote_copy(
            src_ref=src, dst_ref=dst, send_sem=send, recv_sem=recv, device_id=to, device_id_type=MESH
        )

    barrier = pltpu.get_barrier_semaphore()
    for o in range(1, N_ROW):
        pl.semaphore_signal(barrier, inc=1, device_id=(rowdev(o), c), device_id_type=MESH)
    for o in range(1, N_COL):
        pl.semaphore_signal(barrier, inc=1, device_id=(r, (c + o) % N_COL), device_id_type=MESH)

    parts = 8
    size = NBLK // parts
    loads = [
        pltpu.make_async_copy(x_hbm.at[pl.ds(i * size, size)], x.at[pl.ds(i * size, size)], xsem.at[i])
        for i in range(parts)
    ]
    for load in loads:
        load.start()
    x[NBLK] = jnp.zeros((BLK, BLK), bf16)
    xt[NBLK] = jnp.zeros((BLK, BLK), bf16)

    norm = jnp.zeros((DIRS, PIECE), f32)
    for p in range(N_ROW):
        piece = grads[p]
        d[p] = piece
        v[p] = piece.astype(bf16)
        res[p] = piece
        sol[p] = jnp.zeros((DIRS, PIECE), f32)
    mine = grads[r]
    rr[...] = jnp.broadcast_to(total(mine * mine), (8, DIRS))
    for i in range(parts):
        loads[i].wait()

        def turn(b, _, i=i):
            xt[i * size + b] = x[i * size + b].T
            return 0

        lax.fori_loop(0, size, turn, 0, unroll=4)

    pl.semaphore_wait(barrier, N_ROW - 1 + N_COL - 1)

    def iteration(t, _):
        def forward(j):
            out = dot(v[0], tile(xt, table, j, 0, True))
            for p in range(1, N_ROW):
                out += dot(v[p], tile(xt, table, j, p, True))
            return out

        def to_sibling(o):
            return remote(psend.at[t, o], prec.at[t, o], ps.at[t, o], pr.at[t, o], sibling)

        def to_chip(o):
            return remote(csend.at[t, o], crec.at[t, o], cs.at[t, o], cr.at[t, o], (r, chip(o) * 2 + k))

        def summed(o):
            to_sibling(o).wait_recv()
            return pown[o] + prec[t, o].astype(f32)

        def finish(o):
            csend[t, o] = summed(o).astype(bf16)
            to_chip(o).start()

        def step(i, _):
            o = N_CHIP - 1 - i
            psend[t, o] = forward(chip(o) * 2 + 1 - k).astype(bf16)
            to_sibling(o).start()
            pown[o] = forward(chip(o) * 2 + k)

            @pl.when(i > 0)
            def _():
                finish(o + 1)

            return 0

        lax.fori_loop(0, N_CHIP, step, 0)
        rows = summed(0)
        for o in range(N_CHIP - 1, 0, -1):
            to_chip(o).wait_recv()
            rows += crec[t, o].astype(f32)
        s[t, c] = (rows * weights[...]).astype(bf16)

        def direct(o):
            return remote(s.at[t, c], s.at[t, c], ss.at[t, o], sr.at[t, o], (r, chip(o) * 2 + k))

        def direct_in(o):
            j = chip_from(o) * 2 + k
            return remote(s.at[t, j], s.at[t, j], ss.at[t, o], sr.at[t, o], sibling)

        def across(o):
            j = chip_from(o) * 2 + k
            return remote(s.at[t, j], s.at[t, j], fs.at[t, o], fr.at[t, o], sibling)

        def across_in(o):
            j = chip_from(o) * 2 + 1 - k
            return remote(s.at[t, j], s.at[t, j], fs.at[t, o], fr.at[t, o], sibling)

        for o in range(1, N_CHIP):
            direct(o).start()
        across(0).start()

        def image(o):
            return remote(isend.at[t, o], irec.at[t, o], ims.at[t, o], imr.at[t, o], (rowdev(o), c))

        def stage(g):
            for o in (2 * g, 2 * g + 1):
                if o > 0:
                    direct_in(o).wait_recv()
                    across(o).start()

        stage(0)
        for g in range(4):
            if g < 3:
                stage(g + 1)
            for o in (2 * g, 2 * g + 1):
                across_in(o).wait_recv()
            js = [chip_from(o) * 2 + kk for o in (2 * g, 2 * g + 1) for kk in (0, 1)]

            def backward(i, _, g=g, js=js):
                o = (i + 1) % N_ROW
                p = rowdev(o)
                out = dot(s[t, js[0]], tile(x, table, js[0], p, False))
                for j in js[1:]:
                    out += dot(s[t, j], tile(x, table, j, p, False))
                if g > 0:
                    out += acc[o]
                if g < 3:
                    acc[o] = out
                else:

                    @pl.when(i < N_ROW - 1)
                    def _():
                        isend[t, o] = out.astype(bf16)
                        image(o).start()

                    @pl.when(i == N_ROW - 1)
                    def _():
                        acc[0] = out

                return 0

            lax.fori_loop(0, N_ROW, backward, 0)

        features = acc[0]
        for o in range(1, N_ROW):
            image(o).wait_recv()
            features += irec[t, o].astype(f32)
        rounded = features.astype(bf16)
        u[t, r] = rounded
        mine_d = d[r]
        mine_r = res[r]
        w = rounded.astype(f32) + RIDGE * mine_d
        sums = [total(mine_d * w), total(mine_r * w), total(w * w), rr[0:1]]
        sc1[t, 0] = jnp.concatenate(sums + [jnp.zeros((4, DIRS), f32)], axis=0)

        def scalars1(o):
            return remote(sc1.at[t, 0], sc1.at[t, o], s1s.at[t, o], s1r.at[t, o], (r, (c + o) % N_COL))

        def scalars2(o):
            return remote(sc2.at[t, 0], sc2.at[t, o], s2s.at[t, o], s2r.at[t, o], (rowdev(o), c))

        def update_out(o):
            return remote(u.at[t, r], u.at[t, r], us.at[t, o], ur.at[t, o], (rowdev(o), c))

        def update_in(o):
            p = rowdev_from(o)
            return remote(u.at[t, p], u.at[t, p], us.at[t, o], ur.at[t, o], (rowdev(o), c))

        for o in range(1, N_COL):
            scalars1(o).start()
        for o in range(1, N_ROW):
            update_out(o).start()
        both = sc1[t, 0]
        for o in range(1, N_COL):
            scalars1(o).wait_recv()
            both += sc1[t, o]
        sc2[t, 0] = both
        for o in range(1, N_ROW):
            scalars2(o).start()
        for o in range(1, N_ROW):
            scalars2(o).wait_recv()
            both += sc2[t, o]
        curvature, cross, square = both[0:1], both[1:2], both[2:3]
        now = jnp.where(t == 0, both[3:4], rr[0:1])
        alpha = now / curvature
        later = now - 2.0 * alpha * cross + alpha * alpha * square
        rr[...] = jnp.broadcast_to(later, (8, DIRS))
        coef[0] = spread(alpha)
        coef[1] = spread(later / now)

        def update(p):
            piece, alpha, beta = d[p], coef[0], coef[1]
            w = u[t, p].astype(f32) + RIDGE * piece
            sol[p] = sol[p] + alpha * piece
            rest = res[p] - alpha * w
            res[p] = rest
            ahead = rest + beta * piece
            d[p] = ahead
            v[p] = ahead.astype(bf16)

        update(r)
        for o in range(1, N_ROW):
            update_in(o).wait_recv()
            update(rowdev_from(o))
        return 0

    lax.fori_loop(0, ITERS, iteration, 0)

    def drain(t, _):
        for o in range(N_CHIP):
            remote(psend.at[t, o], prec.at[t, o], ps.at[t, o], pr.at[t, o], sibling).wait_send()
            remote(s.at[t, c], s.at[t, c], fs.at[t, o], fr.at[t, o], sibling).wait_send()
        for o in range(1, N_CHIP):
            remote(csend.at[t, o], crec.at[t, o], cs.at[t, o], cr.at[t, o], sibling).wait_send()
            remote(s.at[t, c], s.at[t, c], ss.at[t, o], sr.at[t, o], sibling).wait_send()
            remote(isend.at[t, o], irec.at[t, o], ims.at[t, o], imr.at[t, o], sibling).wait_send()
            remote(u.at[t, r], u.at[t, r], us.at[t, o], ur.at[t, o], sibling).wait_send()
            remote(sc2.at[t, 0], sc2.at[t, o], s2s.at[t, o], s2r.at[t, o], sibling).wait_send()
        for o in range(1, N_COL):
            remote(sc1.at[t, 0], sc1.at[t, o], s1s.at[t, o], s1r.at[t, o], sibling).wait_send()
        return 0

    lax.fori_loop(0, ITERS, drain, 0)


def solve(table, weights, grads, x_blocks):
    vmem = lambda *shape, dtype=bf16: pltpu.VMEM(shape, dtype)
    sems = lambda n: pltpu.SemaphoreType.DMA((ITERS, n))
    piece = (DIRS, PIECE)
    shape = jax.ShapeDtypeStruct((N_ROW, *piece), f32)
    return pl.pallas_call(
        kernel,
        out_shape=(shape, shape),
        in_specs=[
            pl.BlockSpec(memory_space=pltpu.SMEM),
            pl.BlockSpec(memory_space=pltpu.VMEM),
            pl.BlockSpec(memory_space=pltpu.VMEM),
            pl.BlockSpec(memory_space=pl.ANY),
        ],
        out_specs=(pl.BlockSpec(memory_space=pltpu.VMEM), pl.BlockSpec(memory_space=pltpu.VMEM)),
        scratch_shapes=[
            vmem(NBLK + 1, BLK, BLK),
            vmem(NBLK + 1, BLK, BLK),
            vmem(N_ROW, *piece, dtype=f32),
            vmem(N_ROW, *piece),
            vmem(ITERS, N_CHIP, *piece),
            vmem(ITERS, N_CHIP, *piece),
            vmem(N_CHIP, *piece, dtype=f32),
            vmem(ITERS, N_CHIP, *piece),
            vmem(ITERS, N_CHIP, *piece),
            vmem(ITERS, N_COL, *piece),
            vmem(N_ROW, *piece, dtype=f32),
            vmem(ITERS, N_ROW, *piece),
            vmem(ITERS, N_ROW, *piece),
            vmem(ITERS, N_ROW, *piece),
            vmem(ITERS, N_COL, 8, DIRS, dtype=f32),
            vmem(ITERS, N_ROW, 8, DIRS, dtype=f32),
            vmem(8, DIRS, dtype=f32),
            vmem(2, *piece, dtype=f32),
            pltpu.SemaphoreType.DMA((8,)),
            *[sems(8)] * 12,
            *[sems(16)] * 2,
            *[sems(8)] * 2,
        ],
        compiler_params=pltpu.CompilerParams(
            collective_id=0, has_side_effects=True, vmem_limit_bytes=60 * 2**20
        ),
    )(table, weights, grads, x_blocks)


def on_device(x_blocks, block_ids, margins, deleted, grads):
    ids = block_ids[:, 0]
    hit = jnp.arange(RB * FB, dtype=jnp.int32)[:, None] == ids[None, :]
    table = NBLK + jnp.sum(jnp.where(hit, jnp.arange(NBLK, dtype=jnp.int32)[None, :] - NBLK, 0), axis=1)
    r, c = lax.axis_index("row"), lax.axis_index("col")
    own = lax.dynamic_slice_in_dim(margins, c * PIECE, PIECE, 0)
    own_ids = r * margins.shape[0] + c * PIECE + jnp.arange(PIECE, dtype=jnp.int32)
    removed = jnp.any(own_ids[:, None] == deleted[None, :], axis=1)
    logistic = jax.nn.sigmoid(own)
    weights = jnp.where(removed, 0.0, logistic * (1.0 - logistic))[None, :]
    turned = grads.reshape(N_ROW, PIECE, DIRS).transpose(0, 2, 1)
    sol, res = solve(table, weights, turned, x_blocks)
    back = lambda a: a.transpose(0, 2, 1).reshape(N_ROW * PIECE, DIRS)
    return back(sol), back(res)


def solution(mesh):
    in_specs = (P("row", "col", None), P("row", "col"), P("row"), P("row"), P("col", None))
    out_specs = (P("col", None), P("col", None))
    return jax.shard_map(on_device, mesh=mesh, in_specs=in_specs, out_specs=out_specs, check_vma=False)
```

```python
import jax
import jax.numpy as jnp
from jax import lax
from jax.experimental import pallas as pl
from jax.experimental.pallas import tpu as pltpu
from jax.sharding import PartitionSpec as P

ITERS = 3
RIDGE = 0.2
N_ROW, N_COL, N_CHIP = 8, 16, 8
BLK, DIRS, FB, RB, NBLK = 128, 128, 16, 32, 256
PIECE = 256
HALF = DIRS // 2
f32, bf16 = jnp.float32, jnp.bfloat16
MESH = pl.DeviceIdType.MESH


def tile(x, table, j, p, across):
    at = lambda a, b: x[table[(2 * j + a) * FB + 2 * p + b]]
    if across:
        top = jnp.concatenate([at(0, 0), at(1, 0)], axis=1)
        low = jnp.concatenate([at(0, 1), at(1, 1)], axis=1)
    else:
        top = jnp.concatenate([at(0, 0), at(0, 1)], axis=1)
        low = jnp.concatenate([at(1, 0), at(1, 1)], axis=1)
    return jnp.concatenate([top, low], axis=0)


def dot(a, b):
    return jnp.dot(a, b, preferred_element_type=f32)


def totals(one, two):
    fold = lambda a: a[:, :BLK] + a[:, BLK:]
    row = jnp.sum(jnp.concatenate([fold(one), fold(two)], axis=0).T, axis=0, keepdims=True)
    return jnp.broadcast_to(row, (8, DIRS))


def spread(rows):
    square = jnp.broadcast_to(rows[0:1], (DIRS, DIRS)).T
    return square[:HALF], square[HALF:]


def wide(a):
    return jnp.concatenate([a, a], axis=1)


def kernel(
    table, weights, grads, x_hbm, out_sol, out_res,
    x, xt, sol, res, d, v, psend, prec, pown, csend, crec, proj, s, acc, isend, irec, u,
    a1, a2, b1, b2, rr, alpha, beta,
    xsem, ps, pr, cs, cr, fs, fr, ss, sr, ims, imr, us, ur, a1s, a1r, b1s, b1r, a2s, a2r, b2s, b2r,
):
    r, c = lax.axis_index("row"), lax.axis_index("col")
    q, k = c // 2, c % 2
    sibling = (r, q * 2 + 1 - k)

    def chip(o):
        return ((q // 2 + o // 2) % 4) * 2 + (q % 2 + o % 2) % 2

    def chip_from(o):
        return ((q // 2 + 4 - o // 2) % 4) * 2 + (q % 2 + o % 2) % 2

    def rowdev(o):
        return ((r // 4 + o // 4) % 2) * 4 + (r % 4 + o % 4) % 4

    def rowdev_from(o):
        return ((r // 4 + o // 4) % 2) * 4 + (r % 4 + 4 - o % 4) % 4

    def remote(src, dst, send, recv, to):
        return pltpu.make_async_remote_copy(
            src_ref=src, dst_ref=dst, send_sem=send, recv_sem=recv, device_id=to, device_id_type=MESH
        )

    barrier = pltpu.get_barrier_semaphore()
    for o in range(1, N_ROW):
        pl.semaphore_signal(barrier, inc=1, device_id=(rowdev(o), c), device_id_type=MESH)
    for o in range(1, N_COL):
        pl.semaphore_signal(barrier, inc=1, device_id=(r, (c + o) % N_COL), device_id_type=MESH)

    parts = 8
    size = NBLK // parts
    loads = [
        pltpu.make_async_copy(x_hbm.at[pl.ds(i * size, size)], x.at[pl.ds(i * size, size)], xsem.at[i])
        for i in range(parts)
    ]
    for load in loads:
        load.start()
    x[NBLK] = jnp.zeros((BLK, BLK), bf16)
    xt[NBLK] = jnp.zeros((BLK, BLK), bf16)

    zero = jnp.zeros((HALF, PIECE), f32)

    def begin(p, _):
        turned = grads[pl.ds(pl.multiple_of(p * PIECE, PIECE), PIECE), :].T
        for h in range(2):
            piece = turned[h * HALF : (h + 1) * HALF]
            res[h, p] = piece
            v[h, p] = piece.astype(bf16)
            d[h, p] = zero
            sol[h, p] = zero
        return 0

    lax.fori_loop(0, N_ROW, begin, 0)
    for h in range(2):
        proj[h] = zero
        beta[h] = zero
    for i in range(parts):
        loads[i].wait()

        def turn(b, _, i=i):
            xt[i * size + b] = x[i * size + b].T
            return 0

        lax.fori_loop(0, size, turn, 0, unroll=4)

    pl.semaphore_wait(barrier, N_ROW - 1 + N_COL - 1)

    def to_sibling(t, h, o):
        return remote(psend.at[t, h, o], prec.at[t, h, o], ps.at[t, h, o], pr.at[t, h, o], sibling)

    def to_chip(t, h, o):
        return remote(
            csend.at[t, h, o], crec.at[t, h, o], cs.at[t, h, o], cr.at[t, h, o], (r, chip(o) * 2 + k)
        )

    def direct(t, h, o, j):
        return remote(s.at[t, h, j], s.at[t, h, j], ss.at[t, h, o], sr.at[t, h, o], (r, chip(o) * 2 + k))

    def across(t, h, o, j):
        return remote(s.at[t, h, j], s.at[t, h, j], fs.at[t, h, o], fr.at[t, h, o], sibling)

    def image(t, h, o):
        return remote(isend.at[t, h, o], irec.at[t, h, o], ims.at[t, h, o], imr.at[t, h, o], (rowdev(o), c))

    def update(t, h, o, p):
        return remote(u.at[t, h, p], u.at[t, h, p], us.at[t, h, o], ur.at[t, h, o], (rowdev(o), c))

    def along_col(buf, send, recv, t, h, o):
        return remote(
            buf.at[t, h, 0], buf.at[t, h, o], send.at[t, h, o], recv.at[t, h, o], (r, (c + o) % N_COL)
        )

    def along_row(buf, send, recv, t, h, o):
        return remote(buf.at[t, h, 0], buf.at[t, h, o], send.at[t, h, o], recv.at[t, h, o], (rowdev(o), c))

    def share_col(buf, send, recv, t, h, rows):
        buf[t, h, 0] = rows
        for o in range(1, N_COL):
            along_col(buf, send, recv, t, h, o).start()

    def share_row(t, h, buf1, send1, recv1, buf2, send2, recv2):
        rows = buf1[t, h, 0]
        for o in range(1, N_COL):
            along_col(buf1, send1, recv1, t, h, o).wait_recv()
            rows += buf1[t, h, o]
        buf2[t, h, 0] = rows
        for o in range(1, N_ROW):
            along_row(buf2, send2, recv2, t, h, o).start()

    def collect(t, h, buf2, send2, recv2):
        rows = buf2[t, h, 0]
        for o in range(1, N_ROW):
            along_row(buf2, send2, recv2, t, h, o).wait_recv()
            rows += buf2[t, h, o]
        return spread(rows)

    def iteration(t, _):
        def forward(h, _):
            def product(j):
                out = dot(v[h, 0], tile(xt, table, j, 0, True))
                for p in range(1, N_ROW):
                    out += dot(v[h, p], tile(xt, table, j, p, True))
                return out

            def step(i, _):
                o = N_CHIP - 1 - i
                psend[t, h, o] = product(chip(o) * 2 + 1 - k).astype(bf16)
                to_sibling(t, h, o).start()
                pown[h, o] = product(chip(o) * 2 + k)

                @pl.when(i > 0)
                def _():
                    to_sibling(t, h, o + 1).wait_recv()
                    both = pown[h, o + 1] + prec[t, h, o + 1].astype(f32)
                    csend[t, h, o + 1] = both.astype(bf16)
                    to_chip(t, h, o + 1).start()

                return 0

            lax.fori_loop(0, N_CHIP, step, 0)
            return 0

        def rows_done(h, _):
            to_sibling(t, h, 0).wait_recv()
            rows = pown[h, 0] + prec[t, h, 0].astype(f32)

            @pl.when(t > 0)
            def _():
                new, _ = collect(t - 1, h, b2, b2s, b2r)
                beta[h] = wide(new / rr[h])
                rr[h] = new

            for o in range(N_CHIP - 1, 0, -1):
                to_chip(t, h, o).wait_recv()
                rows += crec[t, h, o].astype(f32)
            rows += beta[h] * proj[h]
            proj[h] = rows
            scaled = rows * weights[...]
            s[t, h, c] = scaled.astype(bf16)
            for o in range(1, N_CHIP):
                direct(t, h, o, c).start()
            across(t, h, 0, c).start()
            own = res[h, r]
            ahead = own + beta[h] * d[h, r]
            share_col(a1, a1s, a1r, t, h, totals(scaled * rows + RIDGE * ahead * ahead, own * own))
            return 0

        def backward(h, _):
            def stage(g):
                for o in (2 * g, 2 * g + 1):
                    if o > 0:
                        j = chip_from(o) * 2 + k
                        direct(t, h, o, j).wait_recv()
                        across(t, h, o, j).start()

            stage(0)
            for g in range(4):
                if g < 3:
                    stage(g + 1)
                for o in (2 * g, 2 * g + 1):
                    across(t, h, o, chip_from(o) * 2 + 1 - k).wait_recv()
                js = [chip_from(o) * 2 + kk for o in (2 * g, 2 * g + 1) for kk in (0, 1)]

                def block(i, _, g=g, js=js):
                    o = (i + 1) % N_ROW
                    p = rowdev(o)
                    out = dot(s[t, h, js[0]], tile(x, table, js[0], p, False))
                    for j in js[1:]:
                        out += dot(s[t, h, j], tile(x, table, j, p, False))
                    if g > 0:
                        out += acc[h, o]
                    if g < 3:
                        acc[h, o] = out
                    else:

                        @pl.when(i < N_ROW - 1)
                        def _():
                            isend[t, h, o] = out.astype(bf16)
                            image(t, h, o).start()

                        @pl.when(i == N_ROW - 1)
                        def _():
                            acc[h, 0] = out

                    return 0

                lax.fori_loop(0, N_ROW, block, 0)
                if g == 2:
                    share_row(t, h, a1, a1s, a1r, a2, a2s, a2r)
            return 0

        def features_done(h, _):
            curvature, first = collect(t, h, a2, a2s, a2r)

            @pl.when(t == 0)
            def _():
                rr[h] = first

            alpha[h] = wide(rr[h] / curvature)
            features = acc[h, 0]
            for o in range(1, N_ROW):
                image(t, h, o).wait_recv()
                features += irec[t, h, o].astype(f32)
            rounded = features.astype(bf16)
            u[t, h, r] = rounded
            for o in range(1, N_ROW):
                update(t, h, o, r).start()

            @pl.when(t < ITERS - 1)
            def _():
                own = res[h, r]
                ahead = own + beta[h] * d[h, r]
                own = own - alpha[h] * (u[t, h, r].astype(f32) + RIDGE * ahead)
                share_col(b1, b1s, b1r, t, h, totals(own * own, zero))

            def advance(p, _):
                ahead = res[h, p] + beta[h] * d[h, p]
                d[h, p] = ahead
                sol[h, p] = sol[h, p] + alpha[h] * ahead
                return 0

            lax.fori_loop(0, N_ROW, advance, 0)
            return 0

        def renew(h, _):
            @pl.when(t < ITERS - 1)
            def _():
                share_row(t, h, b1, b1s, b1r, b2, b2s, b2r)

            for o in range(N_ROW):
                p = rowdev_from(o)
                if o > 0:
                    update(t, h, o, p).wait_recv()
                left = res[h, p] - alpha[h] * (u[t, h, p].astype(f32) + RIDGE * d[h, p])
                res[h, p] = left
                v[h, p] = left.astype(bf16)
            return 0

        lax.fori_loop(0, 2, forward, 0)
        lax.fori_loop(0, 2, rows_done, 0)
        lax.fori_loop(0, 2, backward, 0)
        lax.fori_loop(0, 2, features_done, 0)

        @pl.when(t == ITERS - 1)
        def _():
            write(sol, out_sol)

        lax.fori_loop(0, 2, renew, 0)
        return 0

    def write(state, out):
        def turn_back(p, _):
            both = jnp.concatenate([state[0, p], state[1, p]], axis=0)
            out[pl.ds(pl.multiple_of(p * PIECE, PIECE), PIECE), :] = both.T
            return 0

        lax.fori_loop(0, N_ROW, turn_back, 0)

    lax.fori_loop(0, ITERS, iteration, 0)
    write(res, out_res)

    def drain(i, _):
        t, h = i // 2, i % 2
        for o in range(N_CHIP):
            to_sibling(t, h, o).wait_send()
            across(t, h, o, c).wait_send()
        for o in range(1, N_CHIP):
            to_chip(t, h, o).wait_send()
            direct(t, h, o, c).wait_send()
            image(t, h, o).wait_send()
            update(t, h, o, r).wait_send()
            along_row(a2, a2s, a2r, t, h, o).wait_send()
        for o in range(1, N_COL):
            along_col(a1, a1s, a1r, t, h, o).wait_send()

        @pl.when(t < ITERS - 1)
        def _():
            for o in range(1, N_ROW):
                along_row(b2, b2s, b2r, t, h, o).wait_send()
            for o in range(1, N_COL):
                along_col(b1, b1s, b1r, t, h, o).wait_send()

        return 0

    lax.fori_loop(0, 2 * ITERS, drain, 0)


def solve(table, weights, grads, x_blocks):
    vmem = lambda *shape, dtype=bf16: pltpu.VMEM(shape, dtype)
    sems = lambda n: pltpu.SemaphoreType.DMA((ITERS, 2, n))
    piece = (HALF, PIECE)
    shape = jax.ShapeDtypeStruct((N_ROW * PIECE, DIRS), f32)
    return pl.pallas_call(
        kernel,
        out_shape=(shape, shape),
        in_specs=[
            pl.BlockSpec(memory_space=pltpu.SMEM),
            pl.BlockSpec(memory_space=pltpu.VMEM),
            pl.BlockSpec(memory_space=pltpu.VMEM),
            pl.BlockSpec(memory_space=pl.ANY),
        ],
        out_specs=(pl.BlockSpec(memory_space=pltpu.VMEM), pl.BlockSpec(memory_space=pltpu.VMEM)),
        scratch_shapes=[
            vmem(NBLK + 1, BLK, BLK),
            vmem(NBLK + 1, BLK, BLK),
            vmem(2, N_ROW, *piece, dtype=f32),
            vmem(2, N_ROW, *piece, dtype=f32),
            vmem(2, N_ROW, *piece, dtype=f32),
            vmem(2, N_ROW, *piece),
            vmem(ITERS, 2, N_CHIP, *piece),
            vmem(ITERS, 2, N_CHIP, *piece),
            vmem(2, N_CHIP, *piece, dtype=f32),
            vmem(ITERS, 2, N_CHIP, *piece),
            vmem(ITERS, 2, N_CHIP, *piece),
            vmem(2, *piece, dtype=f32),
            vmem(ITERS, 2, N_COL, *piece),
            vmem(2, N_ROW, *piece, dtype=f32),
            vmem(ITERS, 2, N_ROW, *piece),
            vmem(ITERS, 2, N_ROW, *piece),
            vmem(ITERS, 2, N_ROW, *piece),
            vmem(ITERS, 2, N_COL, 8, DIRS, dtype=f32),
            vmem(ITERS, 2, N_ROW, 8, DIRS, dtype=f32),
            vmem(ITERS, 2, N_COL, 8, DIRS, dtype=f32),
            vmem(ITERS, 2, N_ROW, 8, DIRS, dtype=f32),
            vmem(2, HALF, BLK, dtype=f32),
            vmem(2, *piece, dtype=f32),
            vmem(2, *piece, dtype=f32),
            pltpu.SemaphoreType.DMA((8,)),
            *[sems(8)] * 12,
            *[sems(16)] * 4,
            *[sems(8)] * 4,
        ],
        compiler_params=pltpu.CompilerParams(
            collective_id=0, has_side_effects=True, vmem_limit_bytes=60 * 2**20
        ),
    )(table, weights, grads, x_blocks)


def on_device(x_blocks, block_ids, margins, deleted, grads):
    ids = block_ids[:, 0]
    hit = jnp.arange(RB * FB, dtype=jnp.int32)[:, None] == ids[None, :]
    table = NBLK + jnp.sum(jnp.where(hit, jnp.arange(NBLK, dtype=jnp.int32)[None, :] - NBLK, 0), axis=1)
    r, c = lax.axis_index("row"), lax.axis_index("col")
    own = lax.dynamic_slice_in_dim(margins, c * PIECE, PIECE, 0)
    own_ids = r * margins.shape[0] + c * PIECE + jnp.arange(PIECE, dtype=jnp.int32)
    removed = jnp.any(own_ids[:, None] == deleted[None, :], axis=1)
    logistic = jax.nn.sigmoid(own)
    weights = jnp.where(removed, 0.0, logistic * (1.0 - logistic))[None, :]
    return solve(table, weights, grads, x_blocks)


def solution(mesh):
    in_specs = (P("row", "col", None), P("row", "col"), P("row"), P("row"), P("col", None))
    out_specs = (P("col", None), P("col", None))
    return jax.shard_map(on_device, mesh=mesh, in_specs=in_specs, out_specs=out_specs, check_vma=False)
```

```python
import jax
import jax.numpy as jnp
from jax import lax
from jax.experimental import pallas as pl
from jax.experimental.pallas import tpu as pltpu
from jax.sharding import PartitionSpec as P

ITERS = 3
RIDGE = 0.2
N_ROW, N_COL, N_CHIP = 8, 16, 8
BLK, DIRS, FB, RB, NBLK = 128, 128, 16, 32, 256
PIECE = 256
HALF = DIRS // 2
WIDTH = 2
f32, bf16 = jnp.float32, jnp.bfloat16
MESH = pl.DeviceIdType.MESH


def tile(x, table, j, p, across):
    at = lambda a, b: x[table[(2 * j + a) * FB + 2 * p + b]]
    if across:
        top = jnp.concatenate([at(0, 0), at(1, 0)], axis=1)
        low = jnp.concatenate([at(0, 1), at(1, 1)], axis=1)
    else:
        top = jnp.concatenate([at(0, 0), at(0, 1)], axis=1)
        low = jnp.concatenate([at(1, 0), at(1, 1)], axis=1)
    return jnp.concatenate([top, low], axis=0)


def dot(a, b):
    return jnp.dot(a, b, preferred_element_type=f32)


def totals(one, two):
    sums = [jnp.sum((a[:, :BLK] + a[:, BLK:]).T, axis=0, keepdims=True) for a in (one, two)]
    return jnp.concatenate(sums + [jnp.zeros((6, DIRS), f32)], axis=0)


def spread(row):
    square = jnp.broadcast_to(row, (DIRS, DIRS)).T
    return jnp.concatenate([square, square], axis=1)


def kernel(
    table, weights, grads, x_hbm, out_sol, out_res,
    x, xt, sol, res, d, v, psend, prec, pown, csend, crec, proj, s, acc, isend, irec, u,
    a1, a2, b1, b2, rr, alpha, beta,
    xsem, ps, pr, cs, cr, fs, fr, ss, sr, ims, imr, us, ur, a1s, a1r, b1s, b1r, a2s, a2r, b2s, b2r,
):
    r, c = lax.axis_index("row"), lax.axis_index("col")
    q, k = c // 2, c % 2
    sibling = (r, q * 2 + 1 - k)

    def chip(o):
        return ((q // 2 + o // 2) % 4) * 2 + (q % 2 + o % 2) % 2

    def chip_from(o):
        return ((q // 2 + 4 - o // 2) % 4) * 2 + (q % 2 + o % 2) % 2

    def rowdev(o):
        return ((r // 4 + o // 4) % 2) * 4 + (r % 4 + o % 4) % 4

    def rowdev_from(o):
        return ((r // 4 + o // 4) % 2) * 4 + (r % 4 + 4 - o % 4) % 4

    def remote(src, dst, send, recv, to):
        return pltpu.make_async_remote_copy(
            src_ref=src, dst_ref=dst, send_sem=send, recv_sem=recv, device_id=to, device_id_type=MESH
        )

    barrier = pltpu.get_barrier_semaphore()
    for o in range(1, N_ROW):
        pl.semaphore_signal(barrier, inc=1, device_id=(rowdev(o), c), device_id_type=MESH)
    for o in range(1, N_COL):
        pl.semaphore_signal(barrier, inc=1, device_id=(r, (c + o) % N_COL), device_id_type=MESH)

    parts = 8
    size = NBLK // parts
    loads = [
        pltpu.make_async_copy(x_hbm.at[pl.ds(i * size, size)], x.at[pl.ds(i * size, size)], xsem.at[i])
        for i in range(parts)
    ]
    for load in loads:
        load.start()
    x[NBLK] = jnp.zeros((BLK, BLK), bf16)
    xt[NBLK] = jnp.zeros((BLK, BLK), bf16)

    zero = jnp.zeros((DIRS, PIECE), f32)

    def begin(p, _):
        turned = grads[pl.ds(pl.multiple_of(p * PIECE, PIECE), PIECE), :].T
        res[p] = turned
        v[p] = turned.astype(bf16)
        d[p] = zero
        sol[p] = zero
        return 0

    lax.fori_loop(0, N_ROW, begin, 0)
    proj[...] = zero
    beta[...] = zero
    for i in range(parts):
        loads[i].wait()

        def turn(b, _, i=i):
            xt[i * size + b] = x[i * size + b].T
            return 0

        lax.fori_loop(0, size, turn, 0, unroll=4)

    pl.semaphore_wait(barrier, N_ROW - 1 + N_COL - 1)

    def to_sibling(t, o):
        return remote(psend.at[t, o], prec.at[t, o], ps.at[t, o], pr.at[t, o], sibling)

    def to_chip(t, o):
        return remote(csend.at[t, o], crec.at[t, o], cs.at[t, o], cr.at[t, o], (r, chip(o) * 2 + k))

    def direct(t, o, j):
        return remote(s.at[t, j], s.at[t, j], ss.at[t, o], sr.at[t, o], (r, chip(o) * 2 + k))

    def across(t, o, j):
        return remote(s.at[t, j], s.at[t, j], fs.at[t, o], fr.at[t, o], sibling)

    def image(t, h, o):
        return remote(isend.at[t, h, o], irec.at[t, h, o], ims.at[t, h, o], imr.at[t, h, o], (rowdev(o), c))

    def update(t, h, o, p):
        return remote(u.at[t, h, p], u.at[t, h, p], us.at[t, h, o], ur.at[t, h, o], (rowdev(o), c))

    def along_col(buf, send, recv, t, o):
        return remote(buf.at[t, 0], buf.at[t, o], send.at[t, o], recv.at[t, o], (r, (c + o) % N_COL))

    def along_row(buf, send, recv, t, o):
        return remote(buf.at[t, 0], buf.at[t, o], send.at[t, o], recv.at[t, o], (rowdev(o), c))

    def share_col(buf, send, recv, t, rows):
        buf[t, 0] = rows
        for o in range(1, N_COL):
            along_col(buf, send, recv, t, o).start()

    def share_row(t, buf1, send1, recv1, buf2, send2, recv2):
        rows = buf1[t, 0]
        for o in range(1, N_COL):
            along_col(buf1, send1, recv1, t, o).wait_recv()
            rows += buf1[t, o]
        buf2[t, 0] = rows
        for o in range(1, N_ROW):
            along_row(buf2, send2, recv2, t, o).start()

    def collect(t, buf2, send2, recv2):
        rows = buf2[t, 0]
        for o in range(1, N_ROW):
            along_row(buf2, send2, recv2, t, o).wait_recv()
            rows += buf2[t, o]
        return rows

    def iteration(t, _):
        def product(j):
            out = dot(v[0], tile(xt, table, j, 0, True))
            for p in range(1, N_ROW):
                out += dot(v[p], tile(xt, table, j, p, True))
            return out

        def chip_sum(o):
            to_sibling(t, o).wait_recv()
            return pown[o] + prec[t, o].astype(f32)

        def send_sum(o):
            csend[t, o] = chip_sum(o).astype(bf16)
            to_chip(t, o).start()

        def forward(i, _):
            chips = [N_CHIP - 1 - WIDTH * i - w for w in range(WIDTH)]
            theirs = [product(chip(o) * 2 + 1 - k) for o in chips]
            mine = [product(chip(o) * 2 + k) for o in chips]
            for o, piece in zip(chips, theirs):
                psend[t, o] = piece.astype(bf16)
                to_sibling(t, o).start()
            for o, piece in zip(chips, mine):
                pown[o] = piece

            @pl.when(i > 0)
            def _():
                for o in chips:
                    send_sum(o + WIDTH)

            return 0

        lax.fori_loop(0, N_CHIP // WIDTH, forward, 0)
        for o in range(WIDTH - 1, 0, -1):
            send_sum(o)
        rows = chip_sum(0)

        @pl.when(t > 0)
        def _():
            sums = collect(t - 1, b2, b2s, b2r)
            beta[...] = spread(sums[0:1] / rr[0:1])
            rr[...] = jnp.broadcast_to(sums[0:1], (8, DIRS))

        rows += beta[...] * proj[...]
        for o in range(N_CHIP - 1, 0, -1):
            to_chip(t, o).wait_recv()
            rows += crec[t, o].astype(f32)
        scaled = rows * weights[...]
        s[t, c] = scaled.astype(bf16)
        across(t, 0, c).start()
        for o in range(1, N_CHIP):
            direct(t, o, c).start()
        proj[...] = rows
        own = res[r]
        ahead = own + beta[...] * d[r]
        share_col(a1, a1s, a1r, t, totals(scaled * rows + RIDGE * ahead * ahead, own * own))

        def stage(g):
            for o in (2 * g, 2 * g + 1):
                if o > 0:
                    j = chip_from(o) * 2 + k
                    direct(t, o, j).wait_recv()
                    across(t, o, j).start()

        stage(0)
        for g in range(4):
            if g < 3:
                stage(g + 1)
            for o in (2 * g, 2 * g + 1):
                across(t, o, chip_from(o) * 2 + 1 - k).wait_recv()
            js = [chip_from(o) * 2 + kk for o in (2 * g, 2 * g + 1) for kk in (0, 1)]
            outs = []
            for o in range(N_ROW):
                p = rowdev(o)
                out = dot(s[t, js[0]], tile(x, table, js[0], p, False))
                for j in js[1:]:
                    out += dot(s[t, j], tile(x, table, j, p, False))
                outs.append(out)
            for o in range(N_ROW):
                if g > 0:
                    outs[o] += acc[o]
                if g < 3 or o == 0:
                    acc[o] = outs[o]
                else:
                    isend[t, 0, o] = outs[o][:HALF].astype(bf16)
                    isend[t, 1, o] = outs[o][HALF:].astype(bf16)
                    image(t, 0, o).start()
        for o in range(1, N_ROW):
            image(t, 1, o).start()
        share_row(t, a1, a1s, a1r, a2, a2s, a2r)

        for h in range(2):
            half = pl.ds(h * HALF, HALF)
            features = acc[0, half]
            for o in range(1, N_ROW):
                image(t, h, o).wait_recv()
                features += irec[t, h, o].astype(f32)
            u[t, h, r] = features.astype(bf16)
            for o in range(1, N_ROW):
                update(t, h, o, r).start()

        sums = collect(t, a2, a2s, a2r)

        @pl.when(t == 0)
        def _():
            rr[...] = jnp.broadcast_to(sums[1:2], (8, DIRS))

        alpha[...] = spread(rr[0:1] / sums[0:1])

        @pl.when(t < ITERS - 1)
        def _():
            gone = jnp.concatenate([u[t, 0, r], u[t, 1, r]], axis=0).astype(f32)
            own = res[r]
            own = own - alpha[...] * (gone + RIDGE * (own + beta[...] * d[r]))
            share_col(b1, b1s, b1r, t, totals(own * own, zero))

        def advance(p, _):
            ahead = res[p] + beta[...] * d[p]
            d[p] = ahead
            sol[p] = sol[p] + alpha[...] * ahead
            return 0

        lax.fori_loop(0, N_ROW, advance, 0)

        @pl.when(t == ITERS - 1)
        def _():
            write(sol, out_sol)

        for h in range(2):
            half = pl.ds(h * HALF, HALF)

            def renew(o, _, h=h, half=half):
                p = rowdev_from(o)

                @pl.when(o > 0)
                def _():
                    update(t, h, o, p).wait_recv()

                left = res[p, half] - alpha[half] * (u[t, h, p].astype(f32) + RIDGE * d[p, half])
                res[p, half] = left
                v[p, half] = left.astype(bf16)
                return 0

            lax.fori_loop(0, N_ROW, renew, 0)

        @pl.when(t < ITERS - 1)
        def _():
            share_row(t, b1, b1s, b1r, b2, b2s, b2r)

        return 0

    def write(state, out):
        def turn_back(p, _):
            out[pl.ds(pl.multiple_of(p * PIECE, PIECE), PIECE), :] = state[p].T
            return 0

        lax.fori_loop(0, N_ROW, turn_back, 0)

    lax.fori_loop(0, ITERS, iteration, 0)
    write(res, out_res)

    def drain(t, _):
        for o in range(N_CHIP):
            to_sibling(t, o).wait_send()
            across(t, o, c).wait_send()
        for o in range(1, N_CHIP):
            to_chip(t, o).wait_send()
            direct(t, o, c).wait_send()
            along_row(a2, a2s, a2r, t, o).wait_send()
            for h in range(2):
                image(t, h, o).wait_send()
                update(t, h, o, r).wait_send()
        for o in range(1, N_COL):
            along_col(a1, a1s, a1r, t, o).wait_send()

        @pl.when(t < ITERS - 1)
        def _():
            for o in range(1, N_ROW):
                along_row(b2, b2s, b2r, t, o).wait_send()
            for o in range(1, N_COL):
                along_col(b1, b1s, b1r, t, o).wait_send()

        return 0

    lax.fori_loop(0, ITERS, drain, 0)


def solve(table, weights, grads, x_blocks):
    vmem = lambda *shape, dtype=bf16: pltpu.VMEM(shape, dtype)
    sems = lambda *n: pltpu.SemaphoreType.DMA((ITERS, *n))
    piece, half = (DIRS, PIECE), (HALF, PIECE)
    shape = jax.ShapeDtypeStruct((N_ROW * PIECE, DIRS), f32)
    return pl.pallas_call(
        kernel,
        out_shape=(shape, shape),
        in_specs=[
            pl.BlockSpec(memory_space=pltpu.SMEM),
            pl.BlockSpec(memory_space=pltpu.VMEM),
            pl.BlockSpec(memory_space=pltpu.VMEM),
            pl.BlockSpec(memory_space=pl.ANY),
        ],
        out_specs=(pl.BlockSpec(memory_space=pltpu.VMEM), pl.BlockSpec(memory_space=pltpu.VMEM)),
        scratch_shapes=[
            vmem(NBLK + 1, BLK, BLK),
            vmem(NBLK + 1, BLK, BLK),
            vmem(N_ROW, *piece, dtype=f32),
            vmem(N_ROW, *piece, dtype=f32),
            vmem(N_ROW, *piece, dtype=f32),
            vmem(N_ROW, *piece),
            vmem(ITERS, N_CHIP, *piece),
            vmem(ITERS, N_CHIP, *piece),
            vmem(N_CHIP, *piece, dtype=f32),
            vmem(ITERS, N_CHIP, *piece),
            vmem(ITERS, N_CHIP, *piece),
            vmem(*piece, dtype=f32),
            vmem(ITERS, N_COL, *piece),
            vmem(N_ROW, *piece, dtype=f32),
            vmem(ITERS, 2, N_ROW, *half),
            vmem(ITERS, 2, N_ROW, *half),
            vmem(ITERS, 2, N_ROW, *half),
            vmem(ITERS, N_COL, 8, DIRS, dtype=f32),
            vmem(ITERS, N_ROW, 8, DIRS, dtype=f32),
            vmem(ITERS, N_COL, 8, DIRS, dtype=f32),
            vmem(ITERS, N_ROW, 8, DIRS, dtype=f32),
            vmem(8, DIRS, dtype=f32),
            vmem(*piece, dtype=f32),
            vmem(*piece, dtype=f32),
            pltpu.SemaphoreType.DMA((8,)),
            *[sems(8)] * 8,
            *[sems(2, 8)] * 4,
            *[sems(16)] * 4,
            *[sems(8)] * 4,
        ],
        compiler_params=pltpu.CompilerParams(
            collective_id=0, has_side_effects=True, vmem_limit_bytes=60 * 2**20
        ),
    )(table, weights, grads, x_blocks)


def on_device(x_blocks, block_ids, margins, deleted, grads):
    ids = block_ids[:, 0]
    hit = jnp.arange(RB * FB, dtype=jnp.int32)[:, None] == ids[None, :]
    table = NBLK + jnp.sum(jnp.where(hit, jnp.arange(NBLK, dtype=jnp.int32)[None, :] - NBLK, 0), axis=1)
    r, c = lax.axis_index("row"), lax.axis_index("col")
    own = lax.dynamic_slice_in_dim(margins, c * PIECE, PIECE, 0)
    own_ids = r * margins.shape[0] + c * PIECE + jnp.arange(PIECE, dtype=jnp.int32)
    removed = jnp.any(own_ids[:, None] == deleted[None, :], axis=1)
    logistic = jax.nn.sigmoid(own)
    weights = jnp.where(removed, 0.0, logistic * (1.0 - logistic))[None, :]
    return solve(table, weights, grads, x_blocks)


def solution(mesh):
    in_specs = (P("row", "col", None), P("row", "col"), P("row"), P("row"), P("col", None))
    out_specs = (P("col", None), P("col", None))
    return jax.shard_map(on_device, mesh=mesh, in_specs=in_specs, out_specs=out_specs, check_vma=False)
```

```python
import jax
import jax.numpy as jnp
from jax import lax
from jax.experimental import pallas as pl
from jax.experimental.pallas import tpu as pltpu
from jax.sharding import PartitionSpec as P

ITERS = 3
RIDGE = 0.2
N_ROW, N_COL, N_CHIP = 8, 16, 8
BLK, DIRS, FB, RB, NBLK = 128, 128, 16, 32, 256
PIECE = 256
HALF = DIRS // 2
WIDTH = 2
CHIP_ORDER = (5, 1, 3, 7, 4, 2, 6)
ROW_ORDER = (6, 2, 5, 7, 4, 1, 3)
f32, bf16 = jnp.float32, jnp.bfloat16
MESH = pl.DeviceIdType.MESH


def tile(x, table, j, p, across):
    at = lambda a, b: x[table[(2 * j + a) * FB + 2 * p + b]]
    if across:
        top = jnp.concatenate([at(0, 0), at(1, 0)], axis=1)
        low = jnp.concatenate([at(0, 1), at(1, 1)], axis=1)
    else:
        top = jnp.concatenate([at(0, 0), at(0, 1)], axis=1)
        low = jnp.concatenate([at(1, 0), at(1, 1)], axis=1)
    return jnp.concatenate([top, low], axis=0)


def dot(a, b):
    return jnp.dot(a, b, preferred_element_type=f32)


def fold(a):
    return a[:, :BLK] + a[:, BLK:]


def total(parts):
    return jnp.sum(jnp.concatenate([parts[0], parts[1]], axis=0).T, axis=0, keepdims=True)


def packed(rows):
    return jnp.concatenate([*rows, jnp.zeros((8 - len(rows), DIRS), f32)], axis=0)


def spread(row):
    square = jnp.broadcast_to(row, (DIRS, DIRS)).T
    both = jnp.concatenate([square, square], axis=1)
    return both[:HALF], both[HALF:]


def kernel(
    table, weights, grads, x_hbm, out_sol, out_res,
    x, xt, sol, res, d, v, psend, prec, pown, csend, crec, proj, s, acc, isend, irec, u,
    a1, a2, b1, b2, part, rr, alpha, beta,
    xsem, ps, pr, cs, cr, fs, fr, ss, sr, ims, imr, us, ur, a1s, a1r, b1s, b1r, a2s, a2r, b2s, b2r,
):
    r, c = lax.axis_index("row"), lax.axis_index("col")
    q, k = c // 2, c % 2
    sibling = (r, q * 2 + 1 - k)

    def chip(o):
        return ((q // 2 + o // 2) % 4) * 2 + (q % 2 + o % 2) % 2

    def chip_from(o):
        return ((q // 2 + 4 - o // 2) % 4) * 2 + (q % 2 + o % 2) % 2

    def rowdev(o):
        return ((r // 4 + o // 4) % 2) * 4 + (r % 4 + o % 4) % 4

    def rowdev_from(o):
        return ((r // 4 + o // 4) % 2) * 4 + (r % 4 + 4 - o % 4) % 4

    def remote(src, dst, send, recv, to):
        return pltpu.make_async_remote_copy(
            src_ref=src, dst_ref=dst, send_sem=send, recv_sem=recv, device_id=to, device_id_type=MESH
        )

    barrier = pltpu.get_barrier_semaphore()
    for o in range(1, N_ROW):
        pl.semaphore_signal(barrier, inc=1, device_id=(rowdev(o), c), device_id_type=MESH)
    for o in range(1, N_COL):
        pl.semaphore_signal(barrier, inc=1, device_id=(r, (c + o) % N_COL), device_id_type=MESH)

    parts = 8
    size = NBLK // parts
    loads = [
        pltpu.make_async_copy(x_hbm.at[pl.ds(i * size, size)], x.at[pl.ds(i * size, size)], xsem.at[i])
        for i in range(parts)
    ]
    for load in loads:
        load.start()
    x[NBLK] = jnp.zeros((BLK, BLK), bf16)
    xt[NBLK] = jnp.zeros((BLK, BLK), bf16)

    zero = jnp.zeros((HALF, PIECE), f32)

    def begin(p, _):
        turned = grads[pl.ds(pl.multiple_of(p * PIECE, PIECE), PIECE), :].T
        for h in range(2):
            piece = turned[h * HALF : (h + 1) * HALF]
            res[h, p] = piece
            v[h, p] = piece.astype(bf16)
            d[h, p] = zero
            sol[h, p] = zero
        return 0

    lax.fori_loop(0, N_ROW, begin, 0)
    for h in range(2):
        proj[h] = zero
        beta[h] = zero
    for i in range(parts):
        loads[i].wait()

        def turn(b, _, i=i):
            xt[i * size + b] = x[i * size + b].T
            return 0

        lax.fori_loop(0, size, turn, 0, unroll=4)

    pl.semaphore_wait(barrier, N_ROW - 1 + N_COL - 1)

    def to_sibling(t, h, o):
        return remote(psend.at[t, h, o], prec.at[t, h, o], ps.at[t, h, o], pr.at[t, h, o], sibling)

    def to_chip(t, h, o):
        return remote(
            csend.at[t, h, o], crec.at[t, h, o], cs.at[t, h, o], cr.at[t, h, o], (r, chip(o) * 2 + k)
        )

    def direct(t, h, o, j):
        return remote(s.at[t, h, j], s.at[t, h, j], ss.at[t, h, o], sr.at[t, h, o], (r, chip(o) * 2 + k))

    def across(t, h, o, j):
        return remote(s.at[t, h, j], s.at[t, h, j], fs.at[t, h, o], fr.at[t, h, o], sibling)

    def image(t, h, o):
        return remote(isend.at[t, h, o], irec.at[t, h, o], ims.at[t, h, o], imr.at[t, h, o], (rowdev(o), c))

    def update(t, h, o, p):
        return remote(u.at[t, h, p], u.at[t, h, p], us.at[t, h, o], ur.at[t, h, o], (rowdev(o), c))

    def along_col(buf, send, recv, t, o):
        return remote(buf.at[t, 0], buf.at[t, o], send.at[t, o], recv.at[t, o], (r, (c + o) % N_COL))

    def along_row(buf, send, recv, t, o):
        return remote(buf.at[t, 0], buf.at[t, o], send.at[t, o], recv.at[t, o], (rowdev(o), c))

    def share_col(buf, send, recv, t, rows):
        buf[t, 0] = rows
        for o in range(1, N_COL):
            along_col(buf, send, recv, t, o).start()

    def share_row(t, buf1, send1, recv1, buf2, send2, recv2):
        rows = buf1[t, 0]
        for o in range(1, N_COL):
            along_col(buf1, send1, recv1, t, o).wait_recv()
            rows += buf1[t, o]
        buf2[t, 0] = rows
        for o in range(1, N_ROW):
            along_row(buf2, send2, recv2, t, o).start()

    def collect(t, buf2, send2, recv2):
        rows = buf2[t, 0]
        for o in range(1, N_ROW):
            along_row(buf2, send2, recv2, t, o).wait_recv()
            rows += buf2[t, o]
        return rows

    def renew(t, h):
        for o in (0, *ROW_ORDER):
            p = rowdev_from(o)
            if o > 0:
                update(t, h, o, p).wait_recv()
            left = res[h, p] - alpha[h] * (u[t, h, p].astype(f32) + RIDGE * d[h, p])
            res[h, p] = left
            v[h, p] = left.astype(bf16)

    def iteration(t, _):
        def forward(h, _):
            @pl.when((t > 0) & (h > 0))
            def _():
                share_row(t - 1, b1, b1s, b1r, b2, b2s, b2r)

            @pl.when(t > 0)
            def _():
                renew(t - 1, h)

            def product(j):
                out = dot(v[h, 0], tile(xt, table, j, 0, True))
                for p in range(1, N_ROW):
                    out += dot(v[h, p], tile(xt, table, j, p, True))
                return out

            def send_sum(o):
                to_sibling(t, h, o).wait_recv()
                csend[t, h, o] = (pown[h, o] + prec[t, h, o].astype(f32)).astype(bf16)
                to_chip(t, h, o).start()

            order = (*CHIP_ORDER, 0)
            for i in range(0, N_CHIP, WIDTH):
                chips = order[i : i + WIDTH]
                theirs = [product(chip(o) * 2 + 1 - k) for o in chips]
                mine = [product(chip(o) * 2 + k) for o in chips]
                for o, piece in zip(chips, theirs):
                    psend[t, h, o] = piece.astype(bf16)
                    to_sibling(t, h, o).start()
                for o, piece in zip(chips, mine):
                    pown[h, o] = piece
                if i > 0:
                    for o in order[i - WIDTH : i]:
                        send_sum(o)
            for o in order[-WIDTH:-1]:
                send_sum(o)
            return 0

        lax.fori_loop(0, 2, forward, 0)

        @pl.when(t > 0)
        def _():
            new = collect(t - 1, b2, b2s, b2r)[0:1]
            beta[0], beta[1] = spread(new / rr[0:1])
            rr[...] = jnp.broadcast_to(new, (8, DIRS))

        def rows_done(h, _):
            to_sibling(t, h, 0).wait_recv()
            rows = pown[h, 0] + prec[t, h, 0].astype(f32) + beta[h] * proj[h]
            for o in CHIP_ORDER:
                to_chip(t, h, o).wait_recv()
                rows += crec[t, h, o].astype(f32)
            scaled = rows * weights[...]
            s[t, h, c] = scaled.astype(bf16)
            for o in CHIP_ORDER:
                direct(t, h, o, c).start()
            across(t, h, 0, c).start()
            proj[h] = rows
            own = res[h, r]
            ahead = own + beta[h] * d[h, r]
            part[0, h] = fold(scaled * rows + RIDGE * ahead * ahead)
            part[1, h] = fold(own * own)
            return 0

        lax.fori_loop(0, 2, rows_done, 0)
        share_col(a1, a1s, a1r, t, packed([total(part[0]), total(part[1])]))

        def backward(h, _):
            order = (0, *CHIP_ORDER)

            def stage(g):
                for o in order[2 * g : 2 * g + 2]:
                    if o > 0:
                        j = chip_from(o) * 2 + k
                        direct(t, h, o, j).wait_recv()
                        across(t, h, o, j).start()

            stage(0)
            for g in range(4):
                if g < 3:
                    stage(g + 1)
                for o in order[2 * g : 2 * g + 2]:
                    across(t, h, o, chip_from(o) * 2 + 1 - k).wait_recv()
                js = [chip_from(o) * 2 + kk for o in order[2 * g : 2 * g + 2] for kk in (0, 1)]
                outs = []
                rows = (*ROW_ORDER, 0)
                for o in rows:
                    p = rowdev(o)
                    out = dot(s[t, h, js[0]], tile(x, table, js[0], p, False))
                    for j in js[1:]:
                        out += dot(s[t, h, j], tile(x, table, j, p, False))
                    outs.append(out)
                for o, out in zip(rows, outs):
                    if g > 0:
                        out += acc[h, o]
                    if g < 3 or o == 0:
                        acc[h, o] = out
                    else:
                        isend[t, h, o] = out.astype(bf16)
                        image(t, h, o).start()
            return 0

        lax.fori_loop(0, 2, backward, 0)
        share_row(t, a1, a1s, a1r, a2, a2s, a2r)

        def features_done(h, _):
            features = acc[h, 0]
            for o in ROW_ORDER:
                image(t, h, o).wait_recv()
                features += irec[t, h, o].astype(f32)
            u[t, h, r] = features.astype(bf16)
            for o in ROW_ORDER:
                update(t, h, o, r).start()
            return 0

        lax.fori_loop(0, 2, features_done, 0)
        sums = collect(t, a2, a2s, a2r)

        @pl.when(t == 0)
        def _():
            rr[...] = jnp.broadcast_to(sums[1:2], (8, DIRS))

        alpha[0], alpha[1] = spread(rr[0:1] / sums[0:1])

        @pl.when(t < ITERS - 1)
        def _():
            for h in range(2):
                own = res[h, r]
                ahead = own + beta[h] * d[h, r]
                own = own - alpha[h] * (u[t, h, r].astype(f32) + RIDGE * ahead)
                part[0, h] = fold(own * own)
            share_col(b1, b1s, b1r, t, packed([total(part[0])]))

        def advance(i, _):
            h, p = i // N_ROW, i % N_ROW
            ahead = res[h, p] + beta[h] * d[h, p]
            d[h, p] = ahead
            sol[h, p] = sol[h, p] + alpha[h] * ahead
            return 0

        lax.fori_loop(0, 2 * N_ROW, advance, 0, unroll=2)
        return 0

    def write(state, out):
        def turn_back(p, _):
            both = jnp.concatenate([state[0, p], state[1, p]], axis=0)
            out[pl.ds(pl.multiple_of(p * PIECE, PIECE), PIECE), :] = both.T
            return 0

        lax.fori_loop(0, N_ROW, turn_back, 0)

    lax.fori_loop(0, ITERS, iteration, 0)
    write(sol, out_sol)
    for h in range(2):
        renew(ITERS - 1, h)
    write(res, out_res)

    def drain(t, _):
        for h in range(2):
            for o in range(N_CHIP):
                to_sibling(t, h, o).wait_send()
                across(t, h, o, c).wait_send()
            for o in range(1, N_CHIP):
                to_chip(t, h, o).wait_send()
                direct(t, h, o, c).wait_send()
                image(t, h, o).wait_send()
                update(t, h, o, r).wait_send()
        for o in range(1, N_ROW):
            along_row(a2, a2s, a2r, t, o).wait_send()
        for o in range(1, N_COL):
            along_col(a1, a1s, a1r, t, o).wait_send()

        @pl.when(t < ITERS - 1)
        def _():
            for o in range(1, N_ROW):
                along_row(b2, b2s, b2r, t, o).wait_send()
            for o in range(1, N_COL):
                along_col(b1, b1s, b1r, t, o).wait_send()

        return 0

    lax.fori_loop(0, ITERS, drain, 0)


def solve(table, weights, grads, x_blocks):
    vmem = lambda *shape, dtype=bf16: pltpu.VMEM(shape, dtype)
    sems = lambda *n: pltpu.SemaphoreType.DMA((ITERS, *n))
    half = (HALF, PIECE)
    shape = jax.ShapeDtypeStruct((N_ROW * PIECE, DIRS), f32)
    return pl.pallas_call(
        kernel,
        out_shape=(shape, shape),
        in_specs=[
            pl.BlockSpec(memory_space=pltpu.SMEM),
            pl.BlockSpec(memory_space=pltpu.VMEM),
            pl.BlockSpec(memory_space=pltpu.VMEM),
            pl.BlockSpec(memory_space=pl.ANY),
        ],
        out_specs=(pl.BlockSpec(memory_space=pltpu.VMEM), pl.BlockSpec(memory_space=pltpu.VMEM)),
        scratch_shapes=[
            vmem(NBLK + 1, BLK, BLK),
            vmem(NBLK + 1, BLK, BLK),
            vmem(2, N_ROW, *half, dtype=f32),
            vmem(2, N_ROW, *half, dtype=f32),
            vmem(2, N_ROW, *half, dtype=f32),
            vmem(2, N_ROW, *half),
            vmem(ITERS, 2, N_CHIP, *half),
            vmem(ITERS, 2, N_CHIP, *half),
            vmem(2, N_CHIP, *half, dtype=f32),
            vmem(ITERS, 2, N_CHIP, *half),
            vmem(ITERS, 2, N_CHIP, *half),
            vmem(2, *half, dtype=f32),
            vmem(ITERS, 2, N_COL, *half),
            vmem(2, N_ROW, *half, dtype=f32),
            vmem(ITERS, 2, N_ROW, *half),
            vmem(ITERS, 2, N_ROW, *half),
            vmem(ITERS, 2, N_ROW, *half),
            vmem(ITERS, N_COL, 8, DIRS, dtype=f32),
            vmem(ITERS, N_ROW, 8, DIRS, dtype=f32),
            vmem(ITERS, N_COL, 8, DIRS, dtype=f32),
            vmem(ITERS, N_ROW, 8, DIRS, dtype=f32),
            vmem(2, 2, HALF, BLK, dtype=f32),
            vmem(8, DIRS, dtype=f32),
            vmem(2, *half, dtype=f32),
            vmem(2, *half, dtype=f32),
            pltpu.SemaphoreType.DMA((8,)),
            *[sems(2, 8)] * 12,
            *[sems(16)] * 4,
            *[sems(8)] * 4,
        ],
        compiler_params=pltpu.CompilerParams(
            collective_id=0, has_side_effects=True, vmem_limit_bytes=60 * 2**20
        ),
    )(table, weights, grads, x_blocks)


def on_device(x_blocks, block_ids, margins, deleted, grads):
    ids = block_ids[:, 0]
    hit = jnp.arange(RB * FB, dtype=jnp.int32)[:, None] == ids[None, :]
    table = NBLK + jnp.sum(jnp.where(hit, jnp.arange(NBLK, dtype=jnp.int32)[None, :] - NBLK, 0), axis=1)
    r, c = lax.axis_index("row"), lax.axis_index("col")
    own = lax.dynamic_slice_in_dim(margins, c * PIECE, PIECE, 0)
    own_ids = r * margins.shape[0] + c * PIECE + jnp.arange(PIECE, dtype=jnp.int32)
    removed = jnp.any(own_ids[:, None] == deleted[None, :], axis=1)
    logistic = jax.nn.sigmoid(own)
    weights = jnp.where(removed, 0.0, logistic * (1.0 - logistic))[None, :]
    return solve(table, weights, grads, x_blocks)


def solution(mesh):
    in_specs = (P("row", "col", None), P("row", "col"), P("row"), P("row"), P("col", None))
    out_specs = (P("col", None), P("col", None))
    return jax.shard_map(on_device, mesh=mesh, in_specs=in_specs, out_specs=out_specs, check_vma=False)
```

```python
import jax
import jax.numpy as jnp
from jax import lax
from jax.experimental import pallas as pl
from jax.experimental.pallas import tpu as pltpu
from jax.sharding import PartitionSpec as P

ITERS = 3
RIDGE = 0.2
N_ROW, N_COL, N_CHIP = 8, 16, 8
BLK, DIRS, FB, RB, NBLK = 128, 128, 16, 32, 256
DELETED = 512
PIECE = 256
HALF = DIRS // 2
WIDTH = 2
CHIP_ORDER = (5, 1, 3, 7, 4, 2, 6)
ROW_ORDER = (6, 2, 5, 7, 4, 1, 3)
f32, bf16 = jnp.float32, jnp.bfloat16
MESH = pl.DeviceIdType.MESH


def tile(x, table, j, p, across):
    at = lambda a, b: x[table[(2 * j + a) * FB + 2 * p + b]]
    if across:
        top = jnp.concatenate([at(0, 0), at(1, 0)], axis=1)
        low = jnp.concatenate([at(0, 1), at(1, 1)], axis=1)
    else:
        top = jnp.concatenate([at(0, 0), at(0, 1)], axis=1)
        low = jnp.concatenate([at(1, 0), at(1, 1)], axis=1)
    return jnp.concatenate([top, low], axis=0)


def dot(a, b):
    return jnp.dot(a, b, preferred_element_type=f32)


def fold(a):
    return a[:, :BLK] + a[:, BLK:]


def total(parts):
    return jnp.sum(jnp.concatenate([parts[0], parts[1]], axis=0).T, axis=0, keepdims=True)


def packed(rows):
    return jnp.concatenate([*rows, jnp.zeros((8 - len(rows), DIRS), f32)], axis=0)


def spread(row):
    square = jnp.broadcast_to(row, (DIRS, DIRS)).T
    both = jnp.concatenate([square, square], axis=1)
    return both[:HALF], both[HALF:]


def kernel(
    table, margins, deleted, grads, x_hbm, sol, res,
    x, xt, weights, d, v, psend, prec, pown, csend, crec, proj, s, acc, isend, irec, u,
    a1, a2, b1, b2, part, rr, alpha, beta,
    xsem, ps, pr, cs, cr, fs, fr, ss, sr, ims, imr, us, ur, a1s, a1r, b1s, b1r, a2s, a2r, b2s, b2r,
):
    r, c = lax.axis_index("row"), lax.axis_index("col")
    q, k = c // 2, c % 2
    sibling = (r, q * 2 + 1 - k)

    def chip(o):
        return ((q // 2 + o // 2) % 4) * 2 + (q % 2 + o % 2) % 2

    def chip_from(o):
        return ((q // 2 + 4 - o // 2) % 4) * 2 + (q % 2 + o % 2) % 2

    def rowdev(o):
        return ((r // 4 + o // 4) % 2) * 4 + (r % 4 + o % 4) % 4

    def rowdev_from(o):
        return ((r // 4 + o // 4) % 2) * 4 + (r % 4 + 4 - o % 4) % 4

    def remote(src, dst, send, recv, to):
        return pltpu.make_async_remote_copy(
            src_ref=src, dst_ref=dst, send_sem=send, recv_sem=recv, device_id=to, device_id_type=MESH
        )

    barrier = pltpu.get_barrier_semaphore()
    for o in range(1, N_ROW):
        pl.semaphore_signal(barrier, inc=1, device_id=(rowdev(o), c), device_id_type=MESH)
    for o in range(1, N_COL):
        pl.semaphore_signal(barrier, inc=1, device_id=(r, (c + o) % N_COL), device_id_type=MESH)

    parts = 8
    size = NBLK // parts
    loads = [
        pltpu.make_async_copy(x_hbm.at[pl.ds(i * size, size)], x.at[pl.ds(i * size, size)], xsem.at[i])
        for i in range(parts)
    ]
    for load in loads:
        load.start()
    x[NBLK] = jnp.zeros((BLK, BLK), bf16)
    xt[NBLK] = jnp.zeros((BLK, BLK), bf16)

    zero = jnp.zeros((HALF, PIECE), f32)

    def begin(p, _):
        turned = grads[pl.ds(pl.multiple_of(p * PIECE, PIECE), PIECE), :].T
        for h in range(2):
            piece = turned[h * HALF : (h + 1) * HALF]
            res[h, p] = piece
            v[h, p] = piece.astype(bf16)
            d[h, p] = zero
            sol[h, p] = zero
        return 0

    lax.fori_loop(0, N_ROW, begin, 0)
    ids = lax.broadcasted_iota(jnp.int32, (BLK, PIECE), 1) + (r * N_COL + c) * PIECE
    gone = jnp.zeros((BLK, PIECE), f32)
    for i in range(DELETED // BLK):
        listed = jnp.broadcast_to(deleted[:, i * BLK : (i + 1) * BLK].astype(f32), (BLK, BLK)).T
        listed = jnp.concatenate([listed, listed], axis=1)
        gone = jnp.where(listed == ids.astype(f32), 1.0, gone)
    logistic = jax.nn.sigmoid(margins[:, pl.ds(pl.multiple_of(c * PIECE, PIECE), PIECE)])
    weights[...] = jnp.where(jnp.max(gone, axis=0, keepdims=True) > 0.0, 0.0, logistic * (1.0 - logistic))
    for h in range(2):
        proj[h] = zero
        beta[h] = zero
    for i in range(parts):
        loads[i].wait()

        def turn(b, _, i=i):
            xt[i * size + b] = x[i * size + b].T
            return 0

        lax.fori_loop(0, size, turn, 0, unroll=4)

    pl.semaphore_wait(barrier, N_ROW - 1 + N_COL - 1)

    def to_sibling(t, h, o):
        return remote(psend.at[t, h, o], prec.at[t, h, o], ps.at[t, h, o], pr.at[t, h, o], sibling)

    def to_chip(t, h, o):
        return remote(
            csend.at[t, h, o], crec.at[t, h, o], cs.at[t, h, o], cr.at[t, h, o], (r, chip(o) * 2 + k)
        )

    def direct(t, h, o, j):
        return remote(s.at[t, h, j], s.at[t, h, j], ss.at[t, h, o], sr.at[t, h, o], (r, chip(o) * 2 + k))

    def across(t, h, o, j):
        return remote(s.at[t, h, j], s.at[t, h, j], fs.at[t, h, o], fr.at[t, h, o], sibling)

    def image(t, h, o):
        return remote(isend.at[t, h, o], irec.at[t, h, o], ims.at[t, h, o], imr.at[t, h, o], (rowdev(o), c))

    def update(t, h, o, p):
        return remote(u.at[t, h, p], u.at[t, h, p], us.at[t, h, o], ur.at[t, h, o], (rowdev(o), c))

    def along_col(buf, send, recv, t, o):
        return remote(buf.at[t, 0], buf.at[t, o], send.at[t, o], recv.at[t, o], (r, (c + o) % N_COL))

    def along_row(buf, send, recv, t, o):
        return remote(buf.at[t, 0], buf.at[t, o], send.at[t, o], recv.at[t, o], (rowdev(o), c))

    def share_col(buf, send, recv, t, rows):
        buf[t, 0] = rows
        for o in range(1, N_COL):
            along_col(buf, send, recv, t, o).start()

    def share_row(t, buf1, send1, recv1, buf2, send2, recv2):
        rows = buf1[t, 0]
        for o in range(1, N_COL):
            along_col(buf1, send1, recv1, t, o).wait_recv()
            rows += buf1[t, o]
        buf2[t, 0] = rows
        for o in range(1, N_ROW):
            along_row(buf2, send2, recv2, t, o).start()

    def collect(t, buf2, send2, recv2):
        rows = buf2[t, 0]
        for o in range(1, N_ROW):
            along_row(buf2, send2, recv2, t, o).wait_recv()
            rows += buf2[t, o]
        return rows

    def renew(t, h):
        for o in (0, *ROW_ORDER):
            p = rowdev_from(o)
            if o > 0:
                update(t, h, o, p).wait_recv()
            left = res[h, p] - alpha[h] * (u[t, h, p].astype(f32) + RIDGE * d[h, p])
            res[h, p] = left
            v[h, p] = left.astype(bf16)

    def drain(t):
        for h in range(2):
            for o in range(N_CHIP):
                to_sibling(t, h, o).wait_send()
                across(t, h, o, c).wait_send()
            for o in range(1, N_CHIP):
                to_chip(t, h, o).wait_send()
                direct(t, h, o, c).wait_send()
                image(t, h, o).wait_send()
        for o in range(1, N_ROW):
            along_row(a2, a2s, a2r, t, o).wait_send()
        for o in range(1, N_COL):
            along_col(a1, a1s, a1r, t, o).wait_send()

    def drain_updates(t):
        for h in range(2):
            for o in range(1, N_ROW):
                update(t, h, o, r).wait_send()

    def drain_beta(t):
        for o in range(1, N_ROW):
            along_row(b2, b2s, b2r, t, o).wait_send()
        for o in range(1, N_COL):
            along_col(b1, b1s, b1r, t, o).wait_send()

    def iteration(t, _):
        def forward(h, _):
            @pl.when((t > 0) & (h > 0))
            def _():
                share_row(t - 1, b1, b1s, b1r, b2, b2s, b2r)

            @pl.when(t > 0)
            def _():
                renew(t - 1, h)

            def product(j):
                out = dot(v[h, 0], tile(xt, table, j, 0, True))
                for p in range(1, N_ROW):
                    out += dot(v[h, p], tile(xt, table, j, p, True))
                return out

            def send_sum(o):
                to_sibling(t, h, o).wait_recv()
                csend[t, h, o] = (pown[h, o] + prec[t, h, o].astype(f32)).astype(bf16)
                to_chip(t, h, o).start()

            order = (*CHIP_ORDER, 0)
            for i in range(0, N_CHIP, WIDTH):
                chips = order[i : i + WIDTH]
                theirs = [product(chip(o) * 2 + 1 - k) for o in chips]
                mine = [product(chip(o) * 2 + k) for o in chips]
                for o, piece in zip(chips, theirs):
                    psend[t, h, o] = piece.astype(bf16)
                    to_sibling(t, h, o).start()
                for o, piece in zip(chips, mine):
                    pown[h, o] = piece
                if i > 0:
                    for o in order[i - WIDTH : i]:
                        send_sum(o)
            for o in order[-WIDTH:-1]:
                send_sum(o)
            return 0

        lax.fori_loop(0, 2, forward, 0)

        @pl.when(t > 0)
        def _():
            new = collect(t - 1, b2, b2s, b2r)[0:1]
            beta[0], beta[1] = spread(new / rr[0:1])
            rr[...] = jnp.broadcast_to(new, (8, DIRS))

        def rows_done(h, _):
            to_sibling(t, h, 0).wait_recv()
            rows = pown[h, 0] + prec[t, h, 0].astype(f32) + beta[h] * proj[h]
            for o in CHIP_ORDER:
                to_chip(t, h, o).wait_recv()
                rows += crec[t, h, o].astype(f32)
            scaled = rows * weights[...]
            s[t, h, c] = scaled.astype(bf16)
            for o in CHIP_ORDER:
                direct(t, h, o, c).start()
            across(t, h, 0, c).start()
            proj[h] = rows
            own = res[h, r]
            ahead = own + beta[h] * d[h, r]
            part[0, h] = fold(scaled * rows + RIDGE * ahead * ahead)
            part[1, h] = fold(own * own)
            return 0

        lax.fori_loop(0, 2, rows_done, 0)
        share_col(a1, a1s, a1r, t, packed([total(part[0]), total(part[1])]))

        def backward(h, _):
            order = (0, *CHIP_ORDER)

            def stage(g):
                for o in order[2 * g : 2 * g + 2]:
                    if o > 0:
                        j = chip_from(o) * 2 + k
                        direct(t, h, o, j).wait_recv()
                        across(t, h, o, j).start()

            stage(0)
            for g in range(4):
                if g < 3:
                    stage(g + 1)
                for o in order[2 * g : 2 * g + 2]:
                    across(t, h, o, chip_from(o) * 2 + 1 - k).wait_recv()
                js = [chip_from(o) * 2 + kk for o in order[2 * g : 2 * g + 2] for kk in (0, 1)]
                outs = []
                rows = (*ROW_ORDER, 0)
                for o in rows:
                    p = rowdev(o)
                    out = dot(s[t, h, js[0]], tile(x, table, js[0], p, False))
                    for j in js[1:]:
                        out += dot(s[t, h, j], tile(x, table, j, p, False))
                    outs.append(out)
                for o, out in zip(rows, outs):
                    if g > 0:
                        out += acc[h, o]
                    if g < 3 or o == 0:
                        acc[h, o] = out
                    else:
                        isend[t, h, o] = out.astype(bf16)
                        image(t, h, o).start()
            return 0

        lax.fori_loop(0, 2, backward, 0)
        share_row(t, a1, a1s, a1r, a2, a2s, a2r)

        def features_done(h, _):
            features = acc[h, 0]
            for o in ROW_ORDER:
                image(t, h, o).wait_recv()
                features += irec[t, h, o].astype(f32)
            u[t, h, r] = features.astype(bf16)
            for o in ROW_ORDER:
                update(t, h, o, r).start()
            return 0

        lax.fori_loop(0, 2, features_done, 0)
        sums = collect(t, a2, a2s, a2r)

        @pl.when(t == 0)
        def _():
            rr[...] = jnp.broadcast_to(sums[1:2], (8, DIRS))

        alpha[0], alpha[1] = spread(rr[0:1] / sums[0:1])

        @pl.when(t < ITERS - 1)
        def _():
            for h in range(2):
                own = res[h, r]
                ahead = own + beta[h] * d[h, r]
                own = own - alpha[h] * (u[t, h, r].astype(f32) + RIDGE * ahead)
                part[0, h] = fold(own * own)
            share_col(b1, b1s, b1r, t, packed([total(part[0])]))

        def advance(i, _):
            h, p = i // N_ROW, i % N_ROW
            ahead = res[h, p] + beta[h] * d[h, p]
            d[h, p] = ahead
            sol[h, p] = sol[h, p] + alpha[h] * ahead
            return 0

        lax.fori_loop(0, 2 * N_ROW, advance, 0, unroll=2)

        @pl.when(t > 0)
        def _():
            drain_updates(t - 1)
            drain_beta(t - 1)

        drain(t)
        return 0

    lax.fori_loop(0, ITERS, iteration, 0)
    for h in range(2):
        renew(ITERS - 1, h)

    drain_updates(ITERS - 1)


def turn_back(sol, res, out_sol, out_res):
    for state, out in ((sol, out_sol), (res, out_res)):
        for p in range(state.shape[1]):
            out[p * PIECE : (p + 1) * PIECE, :] = jnp.concatenate([state[0, p], state[1, p]], axis=0).T


def turned_back(sol, res):
    shape = jax.ShapeDtypeStruct((N_ROW * PIECE, DIRS), f32)
    steps = 4
    each = N_ROW // steps
    taken = pl.BlockSpec((2, each, HALF, PIECE), lambda i: (0, i, 0, 0))
    given = pl.BlockSpec((each * PIECE, DIRS), lambda i: (i, 0))
    return pl.pallas_call(
        turn_back,
        out_shape=(shape, shape),
        grid=(steps,),
        in_specs=[taken, taken],
        out_specs=(given, given),
    )(sol, res)


def solve(table, margins, deleted, grads, x_blocks):
    vmem = lambda *shape, dtype=bf16: pltpu.VMEM(shape, dtype)
    sems = lambda *n: pltpu.SemaphoreType.DMA((ITERS, *n))
    half = (HALF, PIECE)
    shape = jax.ShapeDtypeStruct((2, N_ROW, *half), f32)
    in_vmem = pl.BlockSpec(memory_space=pltpu.VMEM)
    return pl.pallas_call(
        kernel,
        out_shape=(shape, shape),
        in_specs=[
            pl.BlockSpec(memory_space=pltpu.SMEM),
            in_vmem,
            in_vmem,
            in_vmem,
            pl.BlockSpec(memory_space=pl.ANY),
        ],
        out_specs=(in_vmem, in_vmem),
        scratch_shapes=[
            vmem(NBLK + 1, BLK, BLK),
            vmem(NBLK + 1, BLK, BLK),
            vmem(1, PIECE, dtype=f32),
            vmem(2, N_ROW, *half, dtype=f32),
            vmem(2, N_ROW, *half),
            vmem(ITERS, 2, N_CHIP, *half),
            vmem(ITERS, 2, N_CHIP, *half),
            vmem(2, N_CHIP, *half, dtype=f32),
            vmem(ITERS, 2, N_CHIP, *half),
            vmem(ITERS, 2, N_CHIP, *half),
            vmem(2, *half, dtype=f32),
            vmem(ITERS, 2, N_COL, *half),
            vmem(2, N_ROW, *half, dtype=f32),
            vmem(ITERS, 2, N_ROW, *half),
            vmem(ITERS, 2, N_ROW, *half),
            vmem(ITERS, 2, N_ROW, *half),
            vmem(ITERS, N_COL, 8, DIRS, dtype=f32),
            vmem(ITERS, N_ROW, 8, DIRS, dtype=f32),
            vmem(ITERS, N_COL, 8, DIRS, dtype=f32),
            vmem(ITERS, N_ROW, 8, DIRS, dtype=f32),
            vmem(2, 2, HALF, BLK, dtype=f32),
            vmem(8, DIRS, dtype=f32),
            vmem(2, *half, dtype=f32),
            vmem(2, *half, dtype=f32),
            pltpu.SemaphoreType.DMA((8,)),
            *[sems(2, 8)] * 12,
            *[sems(16)] * 4,
            *[sems(8)] * 4,
        ],
        compiler_params=pltpu.CompilerParams(
            collective_id=0, has_side_effects=True, vmem_limit_bytes=60 * 2**20
        ),
    )(table, margins, deleted, grads, x_blocks)


def on_device(x_blocks, block_ids, margins, deleted, grads):
    hit = jnp.arange(RB * FB, dtype=jnp.int32)[:, None] == block_ids[:, 0][None, :]
    table = jnp.min(jnp.where(hit, jnp.arange(NBLK, dtype=jnp.int32)[None, :], NBLK), axis=1)
    return turned_back(*solve(table, margins[None, :], deleted[None, :], grads, x_blocks))


def solution(mesh):
    in_specs = (P("row", "col", None), P("row", "col"), P("row"), P("row"), P("col", None))
    out_specs = (P("col", None), P("col", None))
    return jax.shard_map(on_device, mesh=mesh, in_specs=in_specs, out_specs=out_specs, check_vma=False)
```

```python
import jax
import jax.numpy as jnp
from jax import lax
from jax.experimental import pallas as pl
from jax.experimental.pallas import tpu as pltpu
from jax.sharding import PartitionSpec as P

ITERS = 3
RIDGE = 0.2
N_ROW, N_COL, N_CHIP = 8, 16, 8
BLK, DIRS, FB, RB, NBLK = 128, 128, 16, 32, 256
DELETED = 512
PIECE = 256
HALF = DIRS // 2
WIDTH = 2
STEPS = 2
CUTS = (0, 3, 6, 8)
CHIP_ORDER = (5, 1, 3, 7, 4, 2, 6)
ROW_ORDER = (6, 2, 5, 7, 4, 1, 3)
f32, bf16 = jnp.float32, jnp.bfloat16
MESH = pl.DeviceIdType.MESH


def tile(x, table, j, p, across):
    at = lambda a, b: x[table[(2 * j + a) * FB + 2 * p + b]]
    if across:
        top = jnp.concatenate([at(0, 0), at(1, 0)], axis=1)
        low = jnp.concatenate([at(0, 1), at(1, 1)], axis=1)
    else:
        top = jnp.concatenate([at(0, 0), at(0, 1)], axis=1)
        low = jnp.concatenate([at(1, 0), at(1, 1)], axis=1)
    return jnp.concatenate([top, low], axis=0)


def dot(a, b):
    return jnp.dot(a, b, preferred_element_type=f32)


def fold(a):
    return a[:, :BLK] + a[:, BLK:]


def total(parts):
    return jnp.sum(jnp.concatenate([parts[0], parts[1]], axis=0).T, axis=0, keepdims=True)


def packed(rows):
    return jnp.concatenate([*rows, jnp.zeros((8 - len(rows), DIRS), f32)], axis=0)


def spread(row):
    square = jnp.broadcast_to(row, (DIRS, DIRS)).T
    both = jnp.concatenate([square, square], axis=1)
    return both[:HALF], both[HALF:]


def kernel(
    table, margins, deleted, grads, x_hbm, out_sol, res,
    x, xt, weights, sol, d, v, psend, prec, pown, csend, crec, proj, s, acc, isend, irec, u,
    a1, a2, b1, b2, part, rr, alpha, beta,
    xsem, ps, pr, cs, cr, fs, fr, ss, sr, ims, imr, us, ur, a1s, a1r, b1s, b1r, a2s, a2r, b2s, b2r,
):
    r, c = lax.axis_index("row"), lax.axis_index("col")
    q, k = c // 2, c % 2
    sibling = (r, q * 2 + 1 - k)

    def chip(o):
        return ((q // 2 + o // 2) % 4) * 2 + (q % 2 + o % 2) % 2

    def chip_from(o):
        return ((q // 2 + 4 - o // 2) % 4) * 2 + (q % 2 + o % 2) % 2

    def rowdev(o):
        return ((r // 4 + o // 4) % 2) * 4 + (r % 4 + o % 4) % 4

    def rowdev_from(o):
        return ((r // 4 + o // 4) % 2) * 4 + (r % 4 + 4 - o % 4) % 4

    def remote(src, dst, send, recv, to):
        return pltpu.make_async_remote_copy(
            src_ref=src, dst_ref=dst, send_sem=send, recv_sem=recv, device_id=to, device_id_type=MESH
        )

    barrier = pltpu.get_barrier_semaphore()
    for o in range(1, N_ROW):
        pl.semaphore_signal(barrier, inc=1, device_id=(rowdev(o), c), device_id_type=MESH)
    for o in range(1, N_COL):
        pl.semaphore_signal(barrier, inc=1, device_id=(r, (c + o) % N_COL), device_id_type=MESH)

    parts = 8
    size = NBLK // parts
    loads = [
        pltpu.make_async_copy(x_hbm.at[pl.ds(i * size, size)], x.at[pl.ds(i * size, size)], xsem.at[i])
        for i in range(parts)
    ]
    for load in loads:
        load.start()
    x[NBLK] = jnp.zeros((BLK, BLK), bf16)
    xt[NBLK] = jnp.zeros((BLK, BLK), bf16)

    zero = jnp.zeros((HALF, PIECE), f32)

    def begin(p, _):
        turned = grads[pl.ds(pl.multiple_of(p * PIECE, PIECE), PIECE), :].T
        for h in range(2):
            piece = turned[h * HALF : (h + 1) * HALF]
            res[h, p] = piece
            v[h, p] = piece.astype(bf16)
            d[h, p] = zero
            sol[h, p] = zero
        return 0

    lax.fori_loop(0, N_ROW, begin, 0)
    ids = lax.broadcasted_iota(jnp.int32, (BLK, PIECE), 1) + (r * N_COL + c) * PIECE
    gone = jnp.zeros((BLK, PIECE), f32)
    for i in range(DELETED // BLK):
        listed = jnp.broadcast_to(deleted[:, i * BLK : (i + 1) * BLK].astype(f32), (BLK, BLK)).T
        listed = jnp.concatenate([listed, listed], axis=1)
        gone = jnp.where(listed == ids.astype(f32), 1.0, gone)
    logistic = jax.nn.sigmoid(margins[:, pl.ds(pl.multiple_of(c * PIECE, PIECE), PIECE)])
    weights[...] = jnp.where(jnp.max(gone, axis=0, keepdims=True) > 0.0, 0.0, logistic * (1.0 - logistic))
    for h in range(2):
        proj[h] = zero
        beta[h] = zero
    for i in range(parts):
        loads[i].wait()

        def turn(b, _, i=i):
            xt[i * size + b] = x[i * size + b].T
            return 0

        lax.fori_loop(0, size, turn, 0, unroll=4)

    pl.semaphore_wait(barrier, N_ROW - 1 + N_COL - 1)

    def to_sibling(t, h, o):
        return remote(psend.at[t, h, o], prec.at[t, h, o], ps.at[t, h, o], pr.at[t, h, o], sibling)

    def to_chip(t, h, o):
        return remote(
            csend.at[t, h, o], crec.at[t, h, o], cs.at[t, h, o], cr.at[t, h, o], (r, chip(o) * 2 + k)
        )

    def direct(t, h, o, j):
        return remote(s.at[t, h, j], s.at[t, h, j], ss.at[t, h, o], sr.at[t, h, o], (r, chip(o) * 2 + k))

    def across(t, h, o, j):
        return remote(s.at[t, h, j], s.at[t, h, j], fs.at[t, h, o], fr.at[t, h, o], sibling)

    def image(t, h, o):
        return remote(isend.at[t, h, o], irec.at[t, h, o], ims.at[t, h, o], imr.at[t, h, o], (rowdev(o), c))

    def update(t, h, o, p):
        return remote(u.at[t, h, p], u.at[t, h, p], us.at[t, h, o], ur.at[t, h, o], (rowdev(o), c))

    def along_col(buf, send, recv, t, o):
        return remote(buf.at[t, 0], buf.at[t, o], send.at[t, o], recv.at[t, o], (r, (c + o) % N_COL))

    def along_row(buf, send, recv, t, o):
        return remote(buf.at[t, 0], buf.at[t, o], send.at[t, o], recv.at[t, o], (rowdev(o), c))

    def share_col(buf, send, recv, t, rows):
        buf[t, 0] = rows
        for o in range(1, N_COL):
            along_col(buf, send, recv, t, o).start()

    def share_row(t, buf1, send1, recv1, buf2, send2, recv2):
        rows = buf1[t, 0]
        for o in range(1, N_COL):
            along_col(buf1, send1, recv1, t, o).wait_recv()
            rows += buf1[t, o]
        buf2[t, 0] = rows
        for o in range(1, N_ROW):
            along_row(buf2, send2, recv2, t, o).start()

    def collect(t, buf2, send2, recv2):
        rows = buf2[t, 0]
        for o in range(1, N_ROW):
            along_row(buf2, send2, recv2, t, o).wait_recv()
            rows += buf2[t, o]
        return rows

    def renew(t, h):
        for o in (0, *ROW_ORDER):
            p = rowdev_from(o)
            if o > 0:
                update(t, h, o, p).wait_recv()
            left = res[h, p] - alpha[h] * (u[t, h, p].astype(f32) + RIDGE * d[h, p])
            res[h, p] = left
            v[h, p] = left.astype(bf16)

    def drain(t):
        for h in range(2):
            for o in range(N_CHIP):
                to_sibling(t, h, o).wait_send()
                across(t, h, o, c).wait_send()
            for o in range(1, N_CHIP):
                to_chip(t, h, o).wait_send()
                direct(t, h, o, c).wait_send()
                image(t, h, o).wait_send()
        for o in range(1, N_ROW):
            along_row(a2, a2s, a2r, t, o).wait_send()
        for o in range(1, N_COL):
            along_col(a1, a1s, a1r, t, o).wait_send()

    def drain_updates(t):
        for h in range(2):
            for o in range(1, N_ROW):
                update(t, h, o, r).wait_send()

    def drain_beta(t):
        for o in range(1, N_ROW):
            along_row(b2, b2s, b2r, t, o).wait_send()
        for o in range(1, N_COL):
            along_col(b1, b1s, b1r, t, o).wait_send()

    def iteration(t, _):
        def forward(h, _):
            @pl.when((t > 0) & (h > 0))
            def _():
                share_row(t - 1, b1, b1s, b1r, b2, b2s, b2r)

            @pl.when(t > 0)
            def _():
                renew(t - 1, h)

            def product(j):
                out = dot(v[h, 0], tile(xt, table, j, 0, True))
                for p in range(1, N_ROW):
                    out += dot(v[h, p], tile(xt, table, j, p, True))
                return out

            def send_sum(o):
                to_sibling(t, h, o).wait_recv()
                csend[t, h, o] = (pown[h, o] + prec[t, h, o].astype(f32)).astype(bf16)
                to_chip(t, h, o).start()

            order = (*CHIP_ORDER, 0)
            for i in range(0, N_CHIP, WIDTH):
                chips = order[i : i + WIDTH]
                theirs = [product(chip(o) * 2 + 1 - k) for o in chips]
                mine = [product(chip(o) * 2 + k) for o in chips]
                for o, piece in zip(chips, theirs):
                    psend[t, h, o] = piece.astype(bf16)
                    to_sibling(t, h, o).start()
                for o, piece in zip(chips, mine):
                    pown[h, o] = piece
                if i > 0:
                    for o in order[i - WIDTH : i]:
                        send_sum(o)
            for o in order[-WIDTH:-1]:
                send_sum(o)
            return 0

        lax.fori_loop(0, 2, forward, 0)

        @pl.when(t > 0)
        def _():
            new = collect(t - 1, b2, b2s, b2r)[0:1]
            beta[0], beta[1] = spread(new / rr[0:1])
            rr[...] = jnp.broadcast_to(new, (8, DIRS))

        def rows_done(h, _):
            to_sibling(t, h, 0).wait_recv()
            rows = pown[h, 0] + prec[t, h, 0].astype(f32) + beta[h] * proj[h]
            for o in CHIP_ORDER:
                to_chip(t, h, o).wait_recv()
                rows += crec[t, h, o].astype(f32)
            scaled = rows * weights[...]
            s[t, h, c] = scaled.astype(bf16)
            for o in CHIP_ORDER:
                direct(t, h, o, c).start()
            across(t, h, 0, c).start()
            proj[h] = rows
            own = res[h, r]
            ahead = own + beta[h] * d[h, r]
            part[0, h] = fold(scaled * rows + RIDGE * ahead * ahead)
            part[1, h] = fold(own * own)
            return 0

        lax.fori_loop(0, 2, rows_done, 0)
        share_col(a1, a1s, a1r, t, packed([total(part[0]), total(part[1])]))

        def backward(h, _):
            order = (0, *CHIP_ORDER)

            def stage(g):
                for o in order[CUTS[g] : CUTS[g + 1]]:
                    if o > 0:
                        j = chip_from(o) * 2 + k
                        direct(t, h, o, j).wait_recv()
                        across(t, h, o, j).start()

            last = len(CUTS) - 2
            stage(0)
            for g in range(last + 1):
                if g < last:
                    stage(g + 1)
                group = order[CUTS[g] : CUTS[g + 1]]
                for o in group:
                    across(t, h, o, chip_from(o) * 2 + 1 - k).wait_recv()
                js = [chip_from(o) * 2 + kk for o in group for kk in (0, 1)]
                outs = []
                rows = (*ROW_ORDER, 0)
                for o in rows:
                    p = rowdev(o)
                    out = dot(s[t, h, js[0]], tile(x, table, js[0], p, False))
                    for j in js[1:]:
                        out += dot(s[t, h, j], tile(x, table, j, p, False))
                    outs.append(out)
                for o, out in zip(rows, outs):
                    if g > 0:
                        out += acc[h, o]
                    if g < last or o == 0:
                        acc[h, o] = out
                    else:
                        isend[t, h, o] = out.astype(bf16)
                        image(t, h, o).start()
            return 0

        lax.fori_loop(0, 2, backward, 0)
        share_row(t, a1, a1s, a1r, a2, a2s, a2r)

        def features_done(h, _):
            features = acc[h, 0]
            for o in ROW_ORDER:
                image(t, h, o).wait_recv()
                features += irec[t, h, o].astype(f32)
            u[t, h, r] = features.astype(bf16)
            for o in ROW_ORDER:
                update(t, h, o, r).start()
            return 0

        lax.fori_loop(0, 2, features_done, 0)
        sums = collect(t, a2, a2s, a2r)

        @pl.when(t == 0)
        def _():
            rr[...] = jnp.broadcast_to(sums[1:2], (8, DIRS))

        alpha[0], alpha[1] = spread(rr[0:1] / sums[0:1])

        @pl.when(t < ITERS - 1)
        def _():
            for h in range(2):
                own = res[h, r]
                ahead = own + beta[h] * d[h, r]
                own = own - alpha[h] * (u[t, h, r].astype(f32) + RIDGE * ahead)
                part[0, h] = fold(own * own)
            share_col(b1, b1s, b1r, t, packed([total(part[0])]))

        def advance(i, _):
            h, p = i // N_ROW, i % N_ROW
            ahead = res[h, p] + beta[h] * d[h, p]
            d[h, p] = ahead
            sol[h, p] = sol[h, p] + alpha[h] * ahead
            return 0

        lax.fori_loop(0, 2 * N_ROW, advance, 0, unroll=2)

        @pl.when(t > 0)
        def _():
            drain_updates(t - 1)
            drain_beta(t - 1)

        @pl.when(t == ITERS - 1)
        def _():
            def turn(p, _):
                both = jnp.concatenate([sol[0, p], sol[1, p]], axis=0)
                out_sol[pl.ds(pl.multiple_of(p * PIECE, PIECE), PIECE), :] = both.T
                return 0

            lax.fori_loop(0, N_ROW, turn, 0)

        drain(t)
        return 0

    lax.fori_loop(0, ITERS, iteration, 0)
    for h in range(2):
        renew(ITERS - 1, h)

    drain_updates(ITERS - 1)


def turn_back(sol, res, out_sol, out_res):
    out_sol[...] = sol[...]
    for p in range(res.shape[1]):
        out_res[p * PIECE : (p + 1) * PIECE, :] = jnp.concatenate([res[0, p], res[1, p]], axis=0).T


def turned_back(sol, res):
    shape = jax.ShapeDtypeStruct((N_ROW * PIECE, DIRS), f32)
    steps = STEPS
    each = N_ROW // steps
    taken = pl.BlockSpec((2, each, HALF, PIECE), lambda i: (0, i, 0, 0))
    given = pl.BlockSpec((each * PIECE, DIRS), lambda i: (i, 0))
    return pl.pallas_call(
        turn_back,
        out_shape=(shape, shape),
        grid=(steps,),
        in_specs=[given, taken],
        out_specs=(given, given),
    )(sol, res)


def solve(table, margins, deleted, grads, x_blocks):
    vmem = lambda *shape, dtype=bf16: pltpu.VMEM(shape, dtype)
    sems = lambda *n: pltpu.SemaphoreType.DMA((ITERS, *n))
    half = (HALF, PIECE)
    shape = jax.ShapeDtypeStruct((2, N_ROW, *half), f32)
    rows = jax.ShapeDtypeStruct((N_ROW * PIECE, DIRS), f32)
    in_vmem = pl.BlockSpec(memory_space=pltpu.VMEM)
    return pl.pallas_call(
        kernel,
        out_shape=(rows, shape),
        in_specs=[
            pl.BlockSpec(memory_space=pltpu.SMEM),
            in_vmem,
            in_vmem,
            in_vmem,
            pl.BlockSpec(memory_space=pl.ANY),
        ],
        out_specs=(in_vmem, in_vmem),
        scratch_shapes=[
            vmem(NBLK + 1, BLK, BLK),
            vmem(NBLK + 1, BLK, BLK),
            vmem(1, PIECE, dtype=f32),
            vmem(2, N_ROW, *half, dtype=f32),
            vmem(2, N_ROW, *half, dtype=f32),
            vmem(2, N_ROW, *half),
            vmem(ITERS, 2, N_CHIP, *half),
            vmem(ITERS, 2, N_CHIP, *half),
            vmem(2, N_CHIP, *half, dtype=f32),
            vmem(ITERS, 2, N_CHIP, *half),
            vmem(ITERS, 2, N_CHIP, *half),
            vmem(2, *half, dtype=f32),
            vmem(ITERS, 2, N_COL, *half),
            vmem(2, N_ROW, *half, dtype=f32),
            vmem(ITERS, 2, N_ROW, *half),
            vmem(ITERS, 2, N_ROW, *half),
            vmem(ITERS, 2, N_ROW, *half),
            vmem(ITERS, N_COL, 8, DIRS, dtype=f32),
            vmem(ITERS, N_ROW, 8, DIRS, dtype=f32),
            vmem(ITERS, N_COL, 8, DIRS, dtype=f32),
            vmem(ITERS, N_ROW, 8, DIRS, dtype=f32),
            vmem(2, 2, HALF, BLK, dtype=f32),
            vmem(8, DIRS, dtype=f32),
            vmem(2, *half, dtype=f32),
            vmem(2, *half, dtype=f32),
            pltpu.SemaphoreType.DMA((8,)),
            *[sems(2, 8)] * 12,
            *[sems(16)] * 4,
            *[sems(8)] * 4,
        ],
        compiler_params=pltpu.CompilerParams(
            collective_id=0, has_side_effects=True, vmem_limit_bytes=60 * 2**20
        ),
    )(table, margins, deleted, grads, x_blocks)


def on_device(x_blocks, block_ids, margins, deleted, grads):
    hit = jnp.arange(RB * FB, dtype=jnp.int32)[:, None] == block_ids[:, 0][None, :]
    table = jnp.min(jnp.where(hit, jnp.arange(NBLK, dtype=jnp.int32)[None, :], NBLK), axis=1)
    return turned_back(*solve(table, margins[None, :], deleted[None, :], grads, x_blocks))


def solution(mesh):
    in_specs = (P("row", "col", None), P("row", "col"), P("row"), P("row"), P("col", None))
    out_specs = (P("col", None), P("col", None))
    return jax.shard_map(on_device, mesh=mesh, in_specs=in_specs, out_specs=out_specs, check_vma=False)
```

```python
import jax
import jax.numpy as jnp
from jax import lax
from jax.experimental import pallas as pl
from jax.experimental.pallas import tpu as pltpu
from jax.sharding import PartitionSpec as P

ITERS = 3
RIDGE = 0.2
N_ROW, N_COL, N_CHIP = 8, 16, 8
BLK, DIRS, FB, RB, NBLK = 128, 128, 16, 32, 256
DELETED = 512
PIECE = 256
HALF = DIRS // 2
WIDTH = 2
STEPS = 1
CUTS = (0, 3, 6, 8)
CHIP_ORDER = (5, 1, 3, 7, 4, 2, 6)
ROW_ORDER = (6, 2, 5, 7, 4, 1, 3)
f32, bf16 = jnp.float32, jnp.bfloat16
MESH = pl.DeviceIdType.MESH


def tile(x, table, j, p, across):
    at = lambda a, b: x[table[(2 * j + a) * FB + 2 * p + b]]
    if across:
        top = jnp.concatenate([at(0, 0), at(1, 0)], axis=1)
        low = jnp.concatenate([at(0, 1), at(1, 1)], axis=1)
    else:
        top = jnp.concatenate([at(0, 0), at(0, 1)], axis=1)
        low = jnp.concatenate([at(1, 0), at(1, 1)], axis=1)
    return jnp.concatenate([top, low], axis=0)


def dot(a, b):
    return jnp.dot(a, b, preferred_element_type=f32)


def fold(a):
    return a[:, :BLK] + a[:, BLK:]


def total(parts):
    return jnp.sum(jnp.concatenate([parts[0], parts[1]], axis=0).T, axis=0, keepdims=True)


def packed(rows):
    return jnp.concatenate([*rows, jnp.zeros((8 - len(rows), DIRS), f32)], axis=0)


def spread(row):
    square = jnp.broadcast_to(row, (DIRS, DIRS)).T
    both = jnp.concatenate([square, square], axis=1)
    return both[:HALF], both[HALF:]


def kernel(
    table, margins, deleted, grads, x_hbm, out_sol, res,
    x, xt, weights, sol, d, v, psend, prec, pown, csend, crec, proj, s, acc, isend, irec, u,
    a1, a2, b1, b2, part, rr, alpha, beta,
    xsem, ps, pr, cs, cr, fs, fr, ss, sr, ims, imr, us, ur, a1s, a1r, b1s, b1r, a2s, a2r, b2s, b2r,
):
    r, c = lax.axis_index("row"), lax.axis_index("col")
    q, k = c // 2, c % 2
    sibling = (r, q * 2 + 1 - k)

    def chip(o):
        return ((q // 2 + o // 2) % 4) * 2 + (q % 2 + o % 2) % 2

    def chip_from(o):
        return ((q // 2 + 4 - o // 2) % 4) * 2 + (q % 2 + o % 2) % 2

    def rowdev(o):
        return ((r // 4 + o // 4) % 2) * 4 + (r % 4 + o % 4) % 4

    def rowdev_from(o):
        return ((r // 4 + o // 4) % 2) * 4 + (r % 4 + 4 - o % 4) % 4

    def remote(src, dst, send, recv, to):
        return pltpu.make_async_remote_copy(
            src_ref=src, dst_ref=dst, send_sem=send, recv_sem=recv, device_id=to, device_id_type=MESH
        )

    barrier = pltpu.get_barrier_semaphore()
    for o in range(1, N_ROW):
        pl.semaphore_signal(barrier, inc=1, device_id=(rowdev(o), c), device_id_type=MESH)
    for o in range(1, N_COL):
        pl.semaphore_signal(barrier, inc=1, device_id=(r, (c + o) % N_COL), device_id_type=MESH)

    parts = 8
    size = NBLK // parts
    loads = [
        pltpu.make_async_copy(x_hbm.at[pl.ds(i * size, size)], x.at[pl.ds(i * size, size)], xsem.at[i])
        for i in range(parts)
    ]
    for load in loads:
        load.start()
    x[NBLK] = jnp.zeros((BLK, BLK), bf16)
    xt[NBLK] = jnp.zeros((BLK, BLK), bf16)

    zero = jnp.zeros((HALF, PIECE), f32)

    def begin(p, _):
        turned = grads[pl.ds(pl.multiple_of(p * PIECE, PIECE), PIECE), :].T
        for h in range(2):
            piece = turned[h * HALF : (h + 1) * HALF]
            res[h, p] = piece
            v[h, p] = piece.astype(bf16)
            d[h, p] = zero
            sol[h, p] = zero
        return 0

    lax.fori_loop(0, N_ROW, begin, 0)
    ids = lax.broadcasted_iota(jnp.int32, (BLK, PIECE), 1) + (r * N_COL + c) * PIECE
    gone = jnp.zeros((BLK, PIECE), f32)
    for i in range(DELETED // BLK):
        listed = jnp.broadcast_to(deleted[:, i * BLK : (i + 1) * BLK].astype(f32), (BLK, BLK)).T
        listed = jnp.concatenate([listed, listed], axis=1)
        gone = jnp.where(listed == ids.astype(f32), 1.0, gone)
    logistic = jax.nn.sigmoid(margins[:, pl.ds(pl.multiple_of(c * PIECE, PIECE), PIECE)])
    weights[...] = jnp.where(jnp.max(gone, axis=0, keepdims=True) > 0.0, 0.0, logistic * (1.0 - logistic))
    for h in range(2):
        proj[h] = zero
        beta[h] = zero
    for i in range(parts):
        loads[i].wait()

        def turn(b, _, i=i):
            xt[i * size + b] = x[i * size + b].T
            return 0

        lax.fori_loop(0, size, turn, 0, unroll=4)

    pl.semaphore_wait(barrier, N_ROW - 1 + N_COL - 1)

    def to_sibling(t, h, o):
        return remote(psend.at[t, h, o], prec.at[t, h, o], ps.at[t, h, o], pr.at[t, h, o], sibling)

    def to_chip(t, h, o):
        return remote(
            csend.at[t, h, o], crec.at[t, h, o], cs.at[t, h, o], cr.at[t, h, o], (r, chip(o) * 2 + k)
        )

    def direct(t, h, o, j):
        return remote(s.at[t, h, j], s.at[t, h, j], ss.at[t, h, o], sr.at[t, h, o], (r, chip(o) * 2 + k))

    def across(t, h, o, j):
        return remote(s.at[t, h, j], s.at[t, h, j], fs.at[t, h, o], fr.at[t, h, o], sibling)

    def image(t, h, o):
        return remote(isend.at[t, h, o], irec.at[t, h, o], ims.at[t, h, o], imr.at[t, h, o], (rowdev(o), c))

    def update(t, h, o, p):
        return remote(u.at[t, h, p], u.at[t, h, p], us.at[t, h, o], ur.at[t, h, o], (rowdev(o), c))

    def along_col(buf, send, recv, t, o):
        return remote(buf.at[t, 0], buf.at[t, o], send.at[t, o], recv.at[t, o], (r, (c + o) % N_COL))

    def along_row(buf, send, recv, t, o):
        return remote(buf.at[t, 0], buf.at[t, o], send.at[t, o], recv.at[t, o], (rowdev(o), c))

    def share_col(buf, send, recv, t, rows):
        buf[t, 0] = rows
        for o in range(1, N_COL):
            along_col(buf, send, recv, t, o).start()

    def share_row(t, buf1, send1, recv1, buf2, send2, recv2):
        rows = buf1[t, 0]
        for o in range(1, N_COL):
            along_col(buf1, send1, recv1, t, o).wait_recv()
            rows += buf1[t, o]
        buf2[t, 0] = rows
        for o in range(1, N_ROW):
            along_row(buf2, send2, recv2, t, o).start()

    def collect(t, buf2, send2, recv2):
        rows = buf2[t, 0]
        for o in range(1, N_ROW):
            along_row(buf2, send2, recv2, t, o).wait_recv()
            rows += buf2[t, o]
        return rows

    def renew(t, h):
        for o in (0, *ROW_ORDER):
            p = rowdev_from(o)
            if o > 0:
                update(t, h, o, p).wait_recv()
            left = res[h, p] - alpha[h] * (u[t, h, p].astype(f32) + RIDGE * d[h, p])
            res[h, p] = left
            v[h, p] = left.astype(bf16)

    def drain(t):
        for h in range(2):
            for o in range(N_CHIP):
                to_sibling(t, h, o).wait_send()
                across(t, h, o, c).wait_send()
            for o in range(1, N_CHIP):
                to_chip(t, h, o).wait_send()
                direct(t, h, o, c).wait_send()
                image(t, h, o).wait_send()
        for o in range(1, N_ROW):
            along_row(a2, a2s, a2r, t, o).wait_send()
        for o in range(1, N_COL):
            along_col(a1, a1s, a1r, t, o).wait_send()

    def drain_updates(t):
        for h in range(2):
            for o in range(1, N_ROW):
                update(t, h, o, r).wait_send()

    def drain_beta(t):
        for o in range(1, N_ROW):
            along_row(b2, b2s, b2r, t, o).wait_send()
        for o in range(1, N_COL):
            along_col(b1, b1s, b1r, t, o).wait_send()

    def iteration(t, _):
        def forward(h, _):
            @pl.when((t > 0) & (h > 0))
            def _():
                share_row(t - 1, b1, b1s, b1r, b2, b2s, b2r)

            @pl.when(t > 0)
            def _():
                renew(t - 1, h)

            def product(j):
                out = dot(v[h, 0], tile(xt, table, j, 0, True))
                for p in range(1, N_ROW):
                    out += dot(v[h, p], tile(xt, table, j, p, True))
                return out

            def send_sum(o):
                to_sibling(t, h, o).wait_recv()
                csend[t, h, o] = (pown[h, o] + prec[t, h, o].astype(f32)).astype(bf16)
                to_chip(t, h, o).start()

            order = (*CHIP_ORDER, 0)
            for i in range(0, N_CHIP, WIDTH):
                chips = order[i : i + WIDTH]
                theirs = [product(chip(o) * 2 + 1 - k) for o in chips]
                mine = [product(chip(o) * 2 + k) for o in chips]
                for o, piece in zip(chips, theirs):
                    psend[t, h, o] = piece.astype(bf16)
                    to_sibling(t, h, o).start()
                for o, piece in zip(chips, mine):
                    pown[h, o] = piece
                if i > 0:
                    for o in order[i - WIDTH : i]:
                        send_sum(o)
            for o in order[-WIDTH:-1]:
                send_sum(o)
            return 0

        lax.fori_loop(0, 2, forward, 0)

        @pl.when(t > 0)
        def _():
            new = collect(t - 1, b2, b2s, b2r)[0:1]
            beta[0], beta[1] = spread(new / rr[0:1])
            rr[...] = jnp.broadcast_to(new, (8, DIRS))

        def rows_done(h, _):
            to_sibling(t, h, 0).wait_recv()
            rows = pown[h, 0] + prec[t, h, 0].astype(f32) + beta[h] * proj[h]
            for o in CHIP_ORDER:
                to_chip(t, h, o).wait_recv()
                rows += crec[t, h, o].astype(f32)
            scaled = rows * weights[...]
            s[t, h, c] = scaled.astype(bf16)
            for o in CHIP_ORDER:
                direct(t, h, o, c).start()
            across(t, h, 0, c).start()
            proj[h] = rows
            own = res[h, r]
            ahead = own + beta[h] * d[h, r]
            part[0, h] = fold(scaled * rows + RIDGE * ahead * ahead)
            part[1, h] = fold(own * own)
            return 0

        lax.fori_loop(0, 2, rows_done, 0)
        share_col(a1, a1s, a1r, t, packed([total(part[0]), total(part[1])]))

        def backward(h, _):
            order = (0, *CHIP_ORDER)

            def stage(g):
                for o in order[CUTS[g] : CUTS[g + 1]]:
                    if o > 0:
                        j = chip_from(o) * 2 + k
                        direct(t, h, o, j).wait_recv()
                        across(t, h, o, j).start()

            last = len(CUTS) - 2
            stage(0)
            for g in range(last + 1):
                if g < last:
                    stage(g + 1)
                group = order[CUTS[g] : CUTS[g + 1]]
                for o in group:
                    across(t, h, o, chip_from(o) * 2 + 1 - k).wait_recv()
                js = [chip_from(o) * 2 + kk for o in group for kk in (0, 1)]
                outs = []
                rows = (*ROW_ORDER, 0)
                for o in rows:
                    p = rowdev(o)
                    out = dot(s[t, h, js[0]], tile(x, table, js[0], p, False))
                    for j in js[1:]:
                        out += dot(s[t, h, j], tile(x, table, j, p, False))
                    outs.append(out)
                for o, out in zip(rows, outs):
                    if g > 0:
                        out += acc[h, o]
                    if g < last or o == 0:
                        acc[h, o] = out
                    else:
                        isend[t, h, o] = out.astype(bf16)
                        image(t, h, o).start()
            return 0

        lax.fori_loop(0, 2, backward, 0)
        share_row(t, a1, a1s, a1r, a2, a2s, a2r)

        def features_done(h, _):
            features = acc[h, 0]
            for o in ROW_ORDER:
                image(t, h, o).wait_recv()
                features += irec[t, h, o].astype(f32)
            u[t, h, r] = features.astype(bf16)
            for o in ROW_ORDER:
                update(t, h, o, r).start()
            return 0

        lax.fori_loop(0, 2, features_done, 0)
        sums = collect(t, a2, a2s, a2r)

        @pl.when(t == 0)
        def _():
            rr[...] = jnp.broadcast_to(sums[1:2], (8, DIRS))

        alpha[0], alpha[1] = spread(rr[0:1] / sums[0:1])

        @pl.when(t < ITERS - 1)
        def _():
            for h in range(2):
                own = res[h, r]
                ahead = own + beta[h] * d[h, r]
                own = own - alpha[h] * (u[t, h, r].astype(f32) + RIDGE * ahead)
                part[0, h] = fold(own * own)
            share_col(b1, b1s, b1r, t, packed([total(part[0])]))

        def advance(i, _):
            h, p = i // N_ROW, i % N_ROW
            ahead = res[h, p] + beta[h] * d[h, p]
            d[h, p] = ahead
            sol[h, p] = sol[h, p] + alpha[h] * ahead
            return 0

        lax.fori_loop(0, 2 * N_ROW, advance, 0, unroll=2)

        @pl.when(t > 0)
        def _():
            drain_updates(t - 1)
            drain_beta(t - 1)

        @pl.when(t == ITERS - 1)
        def _():
            def turn(p, _):
                both = jnp.concatenate([sol[0, p], sol[1, p]], axis=0)
                out_sol[pl.ds(pl.multiple_of(p * PIECE, PIECE), PIECE), :] = both.T
                return 0

            lax.fori_loop(0, N_ROW, turn, 0)

        drain(t)
        return 0

    lax.fori_loop(0, ITERS, iteration, 0)
    for h in range(2):
        renew(ITERS - 1, h)

    drain_updates(ITERS - 1)


def turn_back(sol, res, out_sol, out_res):
    out_sol[...] = sol[...]
    for p in range(res.shape[1]):
        out_res[p * PIECE : (p + 1) * PIECE, :] = jnp.concatenate([res[0, p], res[1, p]], axis=0).T


def turned_back(sol, res):
    shape = jax.ShapeDtypeStruct((N_ROW * PIECE, DIRS), f32)
    steps = STEPS
    each = N_ROW // steps
    taken = pl.BlockSpec((2, each, HALF, PIECE), lambda i: (0, i, 0, 0))
    given = pl.BlockSpec((each * PIECE, DIRS), lambda i: (i, 0))
    return pl.pallas_call(
        turn_back,
        out_shape=(shape, shape),
        grid=(steps,),
        in_specs=[given, taken],
        out_specs=(given, given),
    )(sol, res)


def solve(table, margins, deleted, grads, x_blocks):
    vmem = lambda *shape, dtype=bf16: pltpu.VMEM(shape, dtype)
    sems = lambda *n: pltpu.SemaphoreType.DMA((ITERS, *n))
    half = (HALF, PIECE)
    shape = jax.ShapeDtypeStruct((2, N_ROW, *half), f32)
    rows = jax.ShapeDtypeStruct((N_ROW * PIECE, DIRS), f32)
    in_vmem = pl.BlockSpec(memory_space=pltpu.VMEM)
    return pl.pallas_call(
        kernel,
        out_shape=(rows, shape),
        in_specs=[
            pl.BlockSpec(memory_space=pltpu.SMEM),
            in_vmem,
            in_vmem,
            in_vmem,
            pl.BlockSpec(memory_space=pl.ANY),
        ],
        out_specs=(in_vmem, in_vmem),
        scratch_shapes=[
            vmem(NBLK + 1, BLK, BLK),
            vmem(NBLK + 1, BLK, BLK),
            vmem(1, PIECE, dtype=f32),
            vmem(2, N_ROW, *half, dtype=f32),
            vmem(2, N_ROW, *half, dtype=f32),
            vmem(2, N_ROW, *half),
            vmem(ITERS, 2, N_CHIP, *half),
            vmem(ITERS, 2, N_CHIP, *half),
            vmem(2, N_CHIP, *half, dtype=f32),
            vmem(ITERS, 2, N_CHIP, *half),
            vmem(ITERS, 2, N_CHIP, *half),
            vmem(2, *half, dtype=f32),
            vmem(ITERS, 2, N_COL, *half),
            vmem(2, N_ROW, *half, dtype=f32),
            vmem(ITERS, 2, N_ROW, *half),
            vmem(ITERS, 2, N_ROW, *half),
            vmem(ITERS, 2, N_ROW, *half),
            vmem(ITERS, N_COL, 8, DIRS, dtype=f32),
            vmem(ITERS, N_ROW, 8, DIRS, dtype=f32),
            vmem(ITERS, N_COL, 8, DIRS, dtype=f32),
            vmem(ITERS, N_ROW, 8, DIRS, dtype=f32),
            vmem(2, 2, HALF, BLK, dtype=f32),
            vmem(8, DIRS, dtype=f32),
            vmem(2, *half, dtype=f32),
            vmem(2, *half, dtype=f32),
            pltpu.SemaphoreType.DMA((8,)),
            *[sems(2, 8)] * 12,
            *[sems(16)] * 4,
            *[sems(8)] * 4,
        ],
        compiler_params=pltpu.CompilerParams(
            collective_id=0, has_side_effects=True, vmem_limit_bytes=60 * 2**20
        ),
    )(table, margins, deleted, grads, x_blocks)


def on_device(x_blocks, block_ids, margins, deleted, grads):
    hit = jnp.arange(RB * FB, dtype=jnp.int32)[:, None] == block_ids[:, 0][None, :]
    table = jnp.min(jnp.where(hit, jnp.arange(NBLK, dtype=jnp.int32)[None, :], NBLK), axis=1)
    return turned_back(*solve(table, margins[None, :], deleted[None, :], grads, x_blocks))


def solution(mesh):
    in_specs = (P("row", "col", None), P("row", "col"), P("row"), P("row"), P("col", None))
    out_specs = (P("col", None), P("col", None))
    return jax.shard_map(on_device, mesh=mesh, in_specs=in_specs, out_specs=out_specs, check_vma=False)
```
